128 devices in a mesh: acq: 8 (over y, z_hi), strip: 16 (over z_lo, x, core).
Axes of the slice: x: 4, y: 4, z: 4 (z_hi: 2, z_lo: 2; z = z_hi * 2 + z_lo), core: 2. Of those that a mesh axis runs over, the one named last changes fastest.
Arguments:
- raw_echo_values: float32 [16, 16, 8, 120, 2, 512], P('strip', None, None, 'acq')
- cell_target_line: int32 [16, 16, 8], P('strip'), may hold values from -1 to 63, as said below
- cell_track_displacement: int32 [16, 16, 8], P('strip'), may hold values from -48 to 48
- along_track_chirp_slope: float32 [120], P('acq'), may hold values from 0.001 to 0.01
- along_track_look_radius: int32 [128], P('strip'), may hold values from 5 to 7
- range_look_radius: int32 [64], replicated, may hold values from 3 to 7
Outputs:
- coherence: float32 [120, 120, 2, 8192], P('acq', None, None, 'strip')
The draws below stay inside these ranges and needn't reach their ends.
Inputs may be any that keep to these rules, and one draw needn't show every extreme that they name: `cell_target_line`: in each reader's group of 8 slots for one strip the live slots come first; every row of every strip is named by at least one slot; some groups are full.
All inputs are finite; a program needn't handle non-finite values.
Results may differ from the reference program's by a relative error of at most 0.00065.
Values may be sent and summed in bfloat16 or wider, within the bound.
A program may use at most 320 MiB of HBM per device.

```python
import jax
import jax.numpy as jnp
from jax import lax

ACQ = 120
CS = 64
COLS = 512
OMAX = 48
CAP = 8
NROWS = 1024
OROWS = 128
OCOLS = 64
OPIX = 8192
N_STRIP = 16


def layout(key):
    base = jax.random.fold_in(key, 101)
    keys = jax.random.split(base, 6)
    readers = jnp.arange(N_STRIP, dtype=jnp.int32)
    counts = jax.random.randint(keys[0], (N_STRIP, N_STRIP), CAP // 2, CAP + 1)
    full_reader = jax.random.randint(keys[1], (N_STRIP,), 0, N_STRIP)
    counts = jnp.where(readers[:, None] == full_reader[None, :], CAP, counts)
    full_dest = jax.random.randint(keys[2], (), 0, N_STRIP)
    counts = jnp.where(readers[None, :] == full_dest, CAP, counts)
    small_dest = (full_dest + 1) % N_STRIP
    small_reader = (full_reader[small_dest] + 1) % N_STRIP
    counts = jnp.where((readers[:, None] == small_reader) & (readers[None, :] == small_dest), CAP // 2, counts)
    slots_all = N_STRIP * CAP
    live = jnp.arange(CAP, dtype=jnp.int32)[None, None, :] < counts[:, :, None]
    live_dest = jnp.transpose(live, (1, 0, 2)).reshape(N_STRIP, slots_all)
    orders = jax.vmap(lambda sub: jax.random.permutation(sub, slots_all))(jax.random.split(keys[3], N_STRIP))
    scores = jnp.where(live_dest, orders, orders + slots_all).astype(jnp.int32)
    ranking = jnp.argsort(jnp.argsort(scores, axis=1, stable=True), axis=1, stable=True).astype(jnp.int32)
    extra = jax.random.randint(keys[4], (N_STRIP, slots_all), 0, CS)
    dest = jnp.where(live_dest, jnp.where(ranking < CS, ranking, extra), -1)
    rows = jnp.transpose(dest.reshape(N_STRIP, N_STRIP, CAP), (1, 0, 2)).astype(jnp.int32)
    offsets = jax.random.randint(keys[5], (N_STRIP, N_STRIP, CAP), -OMAX, OMAX + 1)
    offsets = offsets.at[0, 0, 0].set(OMAX).at[0, 0, 1].set(-OMAX)
    return (rows, offsets.astype(jnp.int32))


def ramp(key):
    sub = jax.random.fold_in(key, 202)
    return jnp.exp(jax.random.uniform(sub, (ACQ,), jnp.float32, jnp.log(0.001), jnp.log(0.01)))


def draw_cell_target_line(key, part):
    rows, offsets = layout(key)
    return rows


def draw_cell_track_displacement(key, part):
    rows, offsets = layout(key)
    return offsets


def draw_along_track_chirp_slope(key, part):
    return ramp(key)


def draw_raw_echo_values(key, part):
    rows, offsets = layout(key)
    rates = ramp(key)
    key = jax.random.fold_in(key, 3)
    keys = jax.random.split(key, 3)
    scene = jax.random.normal(keys[0], (N_STRIP, CS, 2, COLS), jnp.float32)
    strips = jnp.arange(N_STRIP, dtype=jnp.int32)[None, :, None]
    common = scene[strips, jnp.clip(rows, 0, CS - 1)]
    gains = jax.random.uniform(keys[1], (ACQ,), jnp.float32, 0.5, 3.0)
    noise = jax.random.normal(keys[2], (N_STRIP, N_STRIP, CAP, ACQ, 2, COLS), jnp.float32)
    value = gains[None, None, None, :, None, None] * common[:, :, :, None] + noise
    phase = (offsets.astype(jnp.float32) ** 2)[..., None] * rates
    cosine = jnp.cos(phase)[..., None]
    sine_part = jnp.sin(phase)[..., None]
    inphase_source = value[..., 0, :]
    quadrature_source = value[..., 1, :]
    real_out = inphase_source * cosine - quadrature_source * sine_part
    imag_out = quadrature_source * cosine + inphase_source * sine_part
    return jnp.stack([real_out, imag_out], axis=-2)


def plant(result, stream_key, least, largest):
    longest = result.shape.index(max(result.shape))
    spots = []
    for shift in (0, 1):
        where = [jax.random.randint(jax.random.fold_in(stream_key, axis), (), 0, length) for axis, length in enumerate(result.shape)]
        where[longest] = (where[longest] + shift) % result.shape[longest]
        spots.append(tuple(where))
    return result.at[spots[0]].set(least).at[spots[1]].set(largest)


def setup_inputs(seed: int = 0) -> dict:
    seeds = jax.random.split(jax.random.key(seed), 7)
    return {
        "raw_echo_values": draw_raw_echo_values(jax.random.fold_in(seeds[6], 71), 0),
        "cell_target_line": draw_cell_target_line(jax.random.fold_in(seeds[6], 71), 0),
        "cell_track_displacement": draw_cell_track_displacement(jax.random.fold_in(seeds[6], 71), 0),
        "along_track_chirp_slope": draw_along_track_chirp_slope(jax.random.fold_in(seeds[6], 71), 0),
        "along_track_look_radius": plant(jax.random.randint(seeds[4], (OROWS,), 5, 8), jax.random.fold_in(seeds[4], 1), 5, 7).astype(jnp.int32),
        "range_look_radius": plant(jax.random.randint(seeds[5], (OCOLS,), 3, 8), jax.random.fold_in(seeds[5], 1), 3, 7).astype(jnp.int32),
    }


epsilon = 1e-06

def subtract_linear_chirp(raw_echo_values, cell_track_displacement, along_track_chirp_slope):
    squared = cell_track_displacement.astype(jnp.float32) ** 2
    phase = squared[..., None] * along_track_chirp_slope
    cosine = jnp.cos(phase)[..., None]
    sine_part = jnp.sin(phase)[..., None]
    inphase_source = raw_echo_values[..., 0, :]
    quadrature_source = raw_echo_values[..., 1, :]
    real_out = inphase_source * cosine + quadrature_source * sine_part
    imag_out = quadrature_source * cosine - inphase_source * sine_part
    return jnp.stack([real_out, imag_out], axis=-2)

def windows_of(padded):
    inner = padded.shape[2] - 8
    acq_count = padded.shape[0]
    columns = padded.shape[3]
    upper = padded[:, :, :inner].reshape(acq_count, 2, inner // 8, 8, columns)
    lower = padded[:, :, 8:].reshape(acq_count, 2, inner // 8, 8, columns)
    return jnp.concatenate([upper, lower], axis=3)

def look(values, colmask):
    return jnp.einsum('...c,cq->...q', values, colmask, precision=lax.Precision.HIGHEST)

def power_of(win, weight):
    return jnp.einsum('apojc,apojc->aoc', win * weight[None, None, :, :, None], win, preferred_element_type=jnp.float32, precision=lax.Precision.HIGHEST)

def coherence_block(left_win, left_power, right_win, weight, colmask):
    weighted = left_win * weight[None, None, :, :, None]
    swapped = jnp.stack([weighted[:, 1], -weighted[:, 0]], axis=1)
    real_sum = jnp.einsum('apojc,bpojc->aboc', weighted, right_win, preferred_element_type=jnp.float32, precision=lax.Precision.HIGHEST)
    imag_sum = jnp.einsum('apojc,bpojc->aboc', swapped, right_win, preferred_element_type=jnp.float32, precision=lax.Precision.HIGHEST)
    right_power = look(power_of(right_win, weight), colmask)
    scale = 1.0 / jnp.sqrt(left_power[:, None] * right_power[None] + epsilon)
    real_look = look(real_sum, colmask) * scale
    imag_look = look(imag_sum, colmask) * scale
    stacked = jnp.stack([real_look, imag_look], axis=2)
    return stacked.reshape(stacked.shape[0], stacked.shape[1], 2, -1)

def make_masks(along_track_look_radius, range_look_radius, columns, out_cols):
    offsets_row = jnp.abs(jnp.arange(16, dtype=jnp.int32) - 8)
    weight = (offsets_row[None, :] <= along_track_look_radius[:, None]).astype(jnp.float32)
    centres = 8 * jnp.arange(out_cols, dtype=jnp.int32) + 4
    distance = jnp.abs(jnp.arange(columns, dtype=jnp.int32)[:, None] - centres[None, :])
    colmask = (distance <= range_look_radius[None, :]).astype(jnp.float32)
    return (weight, colmask)

def reference(raw_echo_values, cell_target_line, cell_track_displacement, along_track_chirp_slope, along_track_look_radius, range_look_radius):
    levelled_echoes = subtract_linear_chirp(raw_echo_values, cell_track_displacement, along_track_chirp_slope).astype(jnp.bfloat16).astype(jnp.float32)
    onehot = (jnp.transpose(cell_target_line, (1, 0, 2))[:, None, :, :] == jnp.arange(CS, dtype=jnp.int32)[None, :, None, None]).astype(jnp.float32)
    counts = lax.optimization_barrier(jnp.sum(onehot, axis=(2, 3)))
    summed = jnp.einsum('sxrk,rskapc->apsxc', onehot, levelled_echoes, precision=lax.Precision.HIGHEST)
    tile = (summed / counts[None, None, :, :, None]).reshape(ACQ, 2, NROWS, COLS).astype(jnp.bfloat16)
    padded = jnp.pad(tile, ((0, 0), (0, 0), (4, 4), (0, 0)))
    weight_all, colmask = make_masks(along_track_look_radius, range_look_radius, COLS, OCOLS)
    per_strip = CS // 8

    def one_strip(index):
        rows = lax.dynamic_slice_in_dim(padded, (index * CS).astype(jnp.int32), CS + 8, 2)
        win = windows_of(rows).astype(jnp.float32)
        weight = lax.dynamic_slice_in_dim(weight_all, (index * per_strip).astype(jnp.int32), per_strip, 0)
        power = look(power_of(win, weight), colmask)
        return coherence_block(win, power, win, weight, colmask)
    blocks = lax.map(one_strip, jnp.arange(N_STRIP, dtype=jnp.int32))
    blocks = blocks.reshape(N_STRIP, ACQ, ACQ, 2, per_strip * OCOLS)
    return jnp.transpose(blocks, (1, 2, 3, 0, 4)).reshape(ACQ, ACQ, 2, OPIX)
```

```python
import jax
import jax.numpy as jnp
from jax import lax
from jax.experimental import pallas as pl
from jax.experimental.pallas import tpu as pltpu
from jax.sharding import PartitionSpec as P

epsilon = 1e-06
N_STRIP = 16
N_GROUP = 8
CAP = 8
ACQ_LOC = 15
PIECE = 2176
ROW_LANE = 2160
CODE = 120.0
VMEM = 56 * 1024 * 1024


def params(limit=VMEM):
    return pltpu.CompilerParams(vmem_limit_bytes=limit)


def pack_kernel(raw_ref, ramp_ref, out_ref):
    ramp = ramp_ref[0]
    lane = lax.broadcasted_iota(jnp.int32, (CAP, 128), 1)
    low = lane < 64
    zero = jnp.zeros((CAP, 128), jnp.float32)
    halo = [[zero, jnp.where(lane == ROW_LANE - 2048, ramp[:, 127:128], 0.0)] for _ in range(N_GROUP)]
    for acq in range(ACQ_LOC):
        cosine = jnp.broadcast_to(ramp[:, acq : acq + 1], (CAP, 128))
        sine = jnp.broadcast_to(ramp[:, 64 + acq : 65 + acq], (CAP, 128))
        tiles = [[], []]
        for t in range(4):
            row = acq * 8 + t * 2
            real = raw_ref[0, pl.ds(row, CAP, stride=ACQ_LOC * 8), :]
            imag = raw_ref[0, pl.ds(row + 1, CAP, stride=ACQ_LOC * 8), :]
            new_real = real * cosine + imag * sine
            new_imag = imag * cosine - real * sine
            tiles[0].append(new_real)
            tiles[1].append(new_imag)
            even = jnp.where(low, new_real, pltpu.roll(new_imag, 64, 1))
            odd = jnp.where(low, pltpu.roll(new_real, 64, 1), new_imag)
            out_ref[2 * t, 0, :, acq * 128 : acq * 128 + 128] = even.astype(jnp.bfloat16)
            out_ref[2 * t + 1, 0, :, acq * 128 : acq * 128 + 128] = odd.astype(jnp.bfloat16)
        for part in range(2):
            vreg = acq // 8
            base = (acq % 8) * 16 + part * 8
            left = (lane >= base) & (lane < base + 4)
            right = (lane >= base + 4) & (lane < base + 8)
            for bound in range(1, N_GROUP):
                t = bound // 2
                if bound % 2:
                    source, start = tiles[part][t], 60
                else:
                    source, start = jnp.where(low, tiles[part][t], tiles[part][t - 1]), 124
                moved = pltpu.roll(source, (base - start) % 128, 1)
                halo[bound][vreg] = jnp.where(left, moved, halo[bound][vreg])
                halo[bound - 1][vreg] = jnp.where(right, moved, halo[bound - 1][vreg])
    for group in range(N_GROUP):
        for vreg in range(2):
            at = ACQ_LOC * 128 + vreg * 128
            out_ref[group, 0, :, at : at + 128] = halo[group][vreg].astype(jnp.bfloat16)


def edge_kernel(slots_ref, out_ref):
    slots = slots_ref[0]
    line = slots[:, ROW_LANE : ROW_LANE + 1].astype(jnp.float32)
    index = lax.broadcasted_iota(jnp.int32, (128, 16), 1)
    wanted = jnp.where(index < 4, index, jnp.where(index < 8, index + 56, 1000)).astype(jnp.float32)
    pick = (line == wanted).astype(jnp.float32).astype(jnp.bfloat16)
    dims = (((0,), (0,)), ((), ()))
    total = lax.dot_general(pick, slots, dims, preferred_element_type=jnp.float32)
    count = lax.dot_general(pick, jnp.ones((128, 128), jnp.bfloat16), dims, preferred_element_type=jnp.float32)
    inverse = 1.0 / jnp.maximum(count[:, :1], 1.0)
    out_ref[0] = (total * inverse).astype(jnp.bfloat16)


def regroup_kernel(slots_ref, before_ref, after_ref, out_ref, lines_ref):
    slots = slots_ref[0]
    line = slots[:, ROW_LANE : ROW_LANE + 1].astype(jnp.float32)
    lane = lax.broadcasted_iota(jnp.int32, (128, 128), 1)
    row = 8 * (lane // 16) + lane % 16 - 4
    inside = (row >= 0) & (row < 64)
    pick = (line == jnp.where(inside, row, 1000).astype(jnp.float32)).astype(jnp.float32)
    lane16 = lax.broadcasted_iota(jnp.int32, (16, 128), 1)
    sub16 = lax.broadcasted_iota(jnp.int32, (16, 128), 0)
    pick_before = ((lane16 < 4) & (sub16 == lane16 + 4)).astype(jnp.float32)
    pick_after = ((lane16 >= 124) & (sub16 == lane16 - 124)).astype(jnp.float32)
    picks = jnp.concatenate([pick, pick_before, pick_after], axis=0)
    inverse = 1.0 / jnp.maximum(jnp.sum(picks, axis=0, keepdims=True), 1.0)
    rows = jnp.concatenate([slots, before_ref[0], after_ref[0]], axis=0)
    total = lax.dot_general(
        rows, picks.astype(jnp.bfloat16), (((0,), (0,)), ((), ())), preferred_element_type=jnp.float32
    )
    lines_ref[...] = total * inverse
    group = lane16 // 16
    for part in range(2):
        for block in range(9):
            v = []
            for c in range(8):
                col = 8 * block + c - 4
                if 0 <= col < 64:
                    at, step = part * 64 + col, 128
                else:
                    at, step = ACQ_LOC * 128 + part * 8 + c, 16
                v.append(lines_ref[pl.ds(at, 16, stride=step), :].astype(jnp.bfloat16))
            for bit in (1, 2, 4):
                clear = (group & bit) == 0
                for i in range(8):
                    if i & bit:
                        continue
                    a, b = v[i], v[i + bit]
                    v[i] = jnp.where(clear, a, pltpu.roll(b, 16 * bit, 1))
                    v[i + bit] = jnp.where(clear, pltpu.roll(a, 128 - 16 * bit, 1), b)
            for o in range(8):
                out_ref[o, part, block] = v[o]


def gram_kernel(win_ref, mask_ref, out_ref):
    row = lax.broadcasted_iota(jnp.int32, (128, 128), 0)
    col = lax.broadcasted_iota(jnp.int32, (128, 128), 1)
    diagonal = row == col
    spare = row % 16 == 15
    dims = (((1,), (1,)), ((), ()))
    for q in range(8):
        re = jnp.concatenate([win_ref[0, 0, q], win_ref[0, 0, q + 1]], axis=1)
        im = jnp.concatenate([win_ref[0, 1, q], win_ref[0, 1, q + 1]], axis=1)
        mask = jnp.concatenate([mask_ref[0, 2 * q : 2 * q + 1, :], mask_ref[0, 2 * q + 1 : 2 * q + 2, :]], axis=1)
        left = jnp.concatenate([re * mask, im * mask], axis=1)
        real = lax.dot_general(left, jnp.concatenate([re, im], axis=1), dims, preferred_element_type=jnp.float32)
        imag = lax.dot_general(left, jnp.concatenate([-im, re], axis=1), dims, preferred_element_type=jnp.float32)
        only = jnp.where(diagonal, real, 0.0)
        power_n = jnp.sum(only, axis=0, keepdims=True)
        power_m = jnp.sum(only, axis=1, keepdims=True)
        scale_n = jnp.where(power_n > 0, lax.rsqrt(power_n), 0.0) * CODE
        scale_m = jnp.where(power_m > 0, lax.rsqrt(power_m), 0.0)
        high = power_n.astype(jnp.bfloat16).astype(jnp.float32)
        code_real = jnp.where(spare, high, jnp.exp2(real * scale_m * scale_n))
        code_imag = jnp.where(spare, power_n - high, jnp.exp2(imag * scale_m * scale_n))
        out_ref[:, q, :, 0:128] = code_real.astype(jnp.bfloat16).reshape(8, 16, 128)
        out_ref[:, q, :, 128:256] = code_imag.astype(jnp.bfloat16).reshape(8, 16, 128)


def place_kernel(code_ref, out_ref, flat_ref, power_ref):
    m = pl.program_id(0)

    @pl.when(m == 0)
    def _():
        for o in range(8):
            for g in range(8):
                at = (o * 64 + g * 8) * 16
                block = code_ref[g, o * 8 : o * 8 + 8].astype(jnp.float32)
                block = block.reshape(128, 256)
                flat_ref[0, at : at + 128, :] = block[:, :128]
                flat_ref[1, at : at + 128, :] = block[:, 128:]
        high = flat_ref[0, pl.ds(15, 512, stride=16), :]
        rest = flat_ref[1, pl.ds(15, 512, stride=16), :]
        power_ref[...] = (high + rest).T

    power_n = power_ref[...]
    me = lax.axis_index("acq") * 16 + m
    power_m = power_ref[pl.ds(me, 1), :]
    scale = jnp.sqrt(power_n) * jnp.sqrt(power_m) * lax.rsqrt(power_n * power_m + epsilon)
    for part in range(2):
        codes = flat_ref[part, pl.ds(m, 512, stride=16), :].T
        scaled = jnp.log2(codes) * (1.0 / CODE) * scale
        for block in range(8):
            for t in range(4):
                piece = scaled[block * 16 : block * 16 + ACQ_LOC, t * 128 : t * 128 + 128]
                out_ref[0, pl.ds(block * ACQ_LOC * 8 + t * 2 + part, ACQ_LOC, stride=8), :] = piece


def per_device(
    raw_echo_values,
    cell_target_line,
    cell_track_displacement,
    along_track_chirp_slope,
    along_track_look_radius,
    range_look_radius,
):
    f32, bf16 = jnp.float32, jnp.bfloat16
    squared = cell_track_displacement[0].astype(f32) ** 2
    phase = squared[..., None] * along_track_chirp_slope
    line = cell_target_line[0].astype(f32)[..., None]
    gap = jnp.zeros((N_STRIP, CAP, 64 - ACQ_LOC), f32)
    ramp = jnp.concatenate([jnp.cos(phase), gap, jnp.sin(phase), gap[..., 1:], line], axis=-1)
    raw = raw_echo_values.reshape(N_STRIP, CAP, ACQ_LOC, 2, 4, 128)
    raw = raw.transpose(0, 1, 2, 4, 3, 5).reshape(N_STRIP, CAP * ACQ_LOC * 8, 128)
    packed = pl.pallas_call(
        pack_kernel,
        grid=(N_STRIP,),
        out_shape=jax.ShapeDtypeStruct((N_GROUP, N_STRIP, CAP, PIECE), bf16),
        in_specs=[
            pl.BlockSpec((1, CAP * ACQ_LOC * 8, 128), lambda s: (s, 0, 0)),
            pl.BlockSpec((1, CAP, 128), lambda s: (s, 0, 0)),
        ],
        out_specs=pl.BlockSpec((N_GROUP, 1, CAP, PIECE), lambda s: (0, s, 0, 0)),
        compiler_params=params(),
        name="pack",
    )(raw, ramp)
    packed = packed.reshape(N_GROUP * N_STRIP, CAP, PIECE)
    slots = lax.all_to_all(packed, ("acq", "strip"), split_axis=0, concat_axis=0, tiled=True)
    slots = slots.reshape(N_GROUP, N_STRIP * CAP, PIECE)
    edges = pl.pallas_call(
        edge_kernel,
        grid=(N_GROUP,),
        out_shape=jax.ShapeDtypeStruct((N_GROUP, 16, PIECE), bf16),
        in_specs=[pl.BlockSpec((1, 128, PIECE), lambda a: (a, 0, 0))],
        out_specs=pl.BlockSpec((1, 16, PIECE), lambda a: (a, 0, 0)),
        compiler_params=params(),
        name="edge",
    )(slots)
    count = lax.axis_size("strip")
    up = [(i, i + 1) for i in range(count - 1)]
    before = lax.ppermute(edges, "strip", up)
    after = lax.ppermute(edges, "strip", [(j, i) for i, j in up])
    windows = pl.pallas_call(
        regroup_kernel,
        grid=(N_GROUP,),
        out_shape=jax.ShapeDtypeStruct((8, 2, 9, 128, 128), bf16),
        in_specs=[
            pl.BlockSpec((1, 128, PIECE), lambda a: (a, 0, 0)),
            pl.BlockSpec((1, 16, PIECE), lambda a: (a, 0, 0)),
            pl.BlockSpec((1, 16, PIECE), lambda a: (a, 0, 0)),
        ],
        out_specs=pl.BlockSpec((8, 2, 9, 16, 128), lambda a: (0, 0, 0, a, 0)),
        scratch_shapes=[pltpu.VMEM((PIECE, 128), f32)],
        compiler_params=params(),
        name="regroup",
    )(slots, before, after)
    group = lax.axis_index("acq")
    radius = lax.dynamic_slice_in_dim(range_look_radius, group * 8, 8, 0)
    across = jnp.arange(16, dtype=jnp.int32)[None, :] - 8
    col_mask = (jnp.abs(across) <= radius[:, None]).reshape(8, 2, 8)
    row_mask = jnp.abs(across) <= along_track_look_radius[:, None]
    masks = (row_mask[:, None, None, None, :] & col_mask[None, :, :, :, None]).reshape(8, 16, 128).astype(bf16)
    codes = pl.pallas_call(
        gram_kernel,
        grid=(8,),
        out_shape=jax.ShapeDtypeStruct((8, 64, 16, 256), bf16),
        in_specs=[
            pl.BlockSpec((1, 2, 9, 128, 128), lambda o: (o, 0, 0, 0, 0)),
            pl.BlockSpec((1, 16, 128), lambda o: (o, 0, 0)),
        ],
        out_specs=pl.BlockSpec((8, 8, 16, 256), lambda o: (0, o, 0, 0)),
        compiler_params=params(),
        name="gram",
    )(windows, masks)
    received = lax.all_to_all(codes, "acq", split_axis=0, concat_axis=0, tiled=True)
    placed = pl.pallas_call(
        place_kernel,
        grid=(ACQ_LOC,),
        out_shape=jax.ShapeDtypeStruct((ACQ_LOC, 960, 128), f32),
        in_specs=[pl.BlockSpec((8, 64, 16, 256), lambda m: (0, 0, 0, 0))],
        out_specs=pl.BlockSpec((1, 960, 128), lambda m: (m, 0, 0)),
        scratch_shapes=[pltpu.VMEM((2, 512 * 16, 128), f32), pltpu.VMEM((128, 512), f32)],
        compiler_params=params(),
        name="place",
    )(received)
    placed = placed.reshape(ACQ_LOC, 120, 4, 2, 128).transpose(0, 1, 3, 2, 4)
    return placed.reshape(ACQ_LOC, 120, 2, 512)


def solution(mesh):
    placed = (
        P("strip", None, None, "acq", None, None),
        P("strip", None, None),
        P("strip", None, None),
        P("acq"),
        P("strip"),
        P(),
    )
    return jax.shard_map(
        per_device,
        mesh=mesh,
        in_specs=placed,
        out_specs=P("acq", None, None, "strip"),
        check_vma=False,
    )
```

```python
import jax
import jax.numpy as jnp
from jax import lax
from jax.experimental import pallas as pl
from jax.experimental.pallas import tpu as pltpu
from jax.sharding import PartitionSpec as P

epsilon = 1e-06
N_STRIP = 16
N_GROUP = 8
CAP = 8
ACQ_LOC = 15
PIECE = 2176
ROW_LANE = 2160
CODE = 120.0
VMEM = 56 * 1024 * 1024


def params(limit=VMEM):
    return pltpu.CompilerParams(vmem_limit_bytes=limit)


def shift(place, strip_step, acq_step):
    acq, strip = place
    dx, dz, dc = (strip_step // 2) % 4, strip_step // 8, strip_step % 2
    dy, dh = acq_step // 2, acq_step % 2
    to_strip = ((strip // 8 + dz) % 2) * 8 + (((strip // 2) % 4 + dx) % 4) * 2 + (strip % 2 + dc) % 2
    to_acq = ((acq // 2 + dy) % 4) * 2 + (acq % 2 + dh) % 2
    return to_acq, to_strip


def strip_step(i):
    return (i * 11) % N_STRIP


def back(step):
    return (step // 8) * 8 + ((4 - (step // 2) % 4) % 4) * 2 + step % 2


def acq_step(n):
    half, rest = n // 4, n % 4
    dy = (1 - half) * (rest // 2) * 2 + half * (1 + 2 * (rest % 2))
    dh = (1 - half) * (rest % 2) + half * (rest // 2)
    return dy * 2 + dh


def acq_back(step):
    return ((4 - step // 2) % 4) * 2 + step % 2


def pack_tile(raw_ref, ramp_ref, packed_ref, s, t):
    ramp = ramp_ref[s]
    lane = lax.broadcasted_iota(jnp.int32, (CAP, 128), 1)
    low = lane < 64
    left_tile, right_tile = (t + 3) % 4, (t + 1) % 4
    kept = jnp.where(low, jnp.where(t < 3, 1.0, 0.0), jnp.where(t > 0, 1.0, 0.0))
    zero = jnp.zeros((CAP, 128), jnp.float32)
    line = jnp.where(lane == ROW_LANE - 2048, ramp[:, 127:128], 0.0)
    halo = [[zero, line], [zero, line]]

    def load(a, tile, part):
        return raw_ref[s, pl.ds(a * 8 + tile * 2 + part, CAP, stride=ACQ_LOC * 8), :]

    for a in range(ACQ_LOC):
        cosine = jnp.broadcast_to(ramp[:, a : a + 1], (CAP, 128))
        sine = jnp.broadcast_to(ramp[:, 64 + a : 65 + a], (CAP, 128))
        real, imag = load(a, t, 0), load(a, t, 1)
        main = [real * cosine + imag * sine, imag * cosine - real * sine]
        real = jnp.where(low, load(a, right_tile, 0), load(a, left_tile, 0)) * kept
        imag = jnp.where(low, load(a, right_tile, 1), load(a, left_tile, 1)) * kept
        outer = [real * cosine + imag * sine, imag * cosine - real * sine]
        even = jnp.where(low, main[0], pltpu.roll(main[1], 64, 1))
        odd = jnp.where(low, pltpu.roll(main[0], 64, 1), main[1])
        packed_ref[2 * t, s, :, a * 128 : a * 128 + 128] = even.astype(jnp.bfloat16)
        packed_ref[2 * t + 1, s, :, a * 128 : a * 128 + 128] = odd.astype(jnp.bfloat16)
        vreg = a // 8
        for part in range(2):
            base = (a % 8) * 16 + part * 8
            left = (lane >= base) & (lane < base + 4)
            right = (lane >= base + 4) & (lane < base + 8)
            inner = pltpu.roll(main[part], (base - 60) % 128, 1)
            edge = pltpu.roll(outer[part], (base - 124) % 128, 1)
            halo[0][vreg] = jnp.where(left, edge, jnp.where(right, inner, halo[0][vreg]))
            halo[1][vreg] = jnp.where(left, inner, jnp.where(right, edge, halo[1][vreg]))
    for side in range(2):
        for vreg in range(2):
            at = ACQ_LOC * 128 + vreg * 128
            packed_ref[2 * t + side, s, :, at : at + 128] = halo[side][vreg].astype(jnp.bfloat16)


def edge_rows(slots):
    line = slots[:, ROW_LANE : ROW_LANE + 1].astype(jnp.float32)
    index = lax.broadcasted_iota(jnp.int32, (128, 16), 1)
    wanted = jnp.where(index < 4, index, jnp.where(index < 8, index + 56, 1000)).astype(jnp.float32)
    pick = (line == wanted).astype(jnp.float32).astype(jnp.bfloat16)
    dims = (((0,), (0,)), ((), ()))
    total = lax.dot_general(pick, slots, dims, preferred_element_type=jnp.float32)
    count = lax.dot_general(pick, jnp.ones((128, 128), jnp.bfloat16), dims, preferred_element_type=jnp.float32)
    inverse = 1.0 / jnp.maximum(count[:, :1], 1.0)
    return (total * inverse).astype(jnp.bfloat16)


def regroup(slots, before, after, has_before, has_after, lines_ref, store):
    line = slots[:, ROW_LANE : ROW_LANE + 1].astype(jnp.float32)
    lane = lax.broadcasted_iota(jnp.int32, (128, 128), 1)
    row = 8 * (lane // 16) + lane % 16 - 4
    inside = (row >= 0) & (row < 64)
    pick = (line == jnp.where(inside, row, 1000).astype(jnp.float32)).astype(jnp.float32)
    lane16 = lax.broadcasted_iota(jnp.int32, (16, 128), 1)
    sub16 = lax.broadcasted_iota(jnp.int32, (16, 128), 0)
    pick_before = ((lane16 < 4) & (sub16 == lane16 + 4)).astype(jnp.float32) * has_before
    pick_after = ((lane16 >= 124) & (sub16 == lane16 - 124)).astype(jnp.float32) * has_after
    picks = jnp.concatenate([pick, pick_before, pick_after], axis=0)
    inverse = 1.0 / jnp.maximum(jnp.sum(picks, axis=0, keepdims=True), 1.0)
    rows = jnp.concatenate([slots, before, after], axis=0)
    total = lax.dot_general(
        rows, picks.astype(jnp.bfloat16), (((0,), (0,)), ((), ())), preferred_element_type=jnp.float32
    )
    lines_ref[...] = total * inverse
    group = lane16 // 16
    for part in range(2):
        for block in range(9):
            v = []
            for c in range(8):
                col = 8 * block + c - 4
                if 0 <= col < 64:
                    at, step = part * 64 + col, 128
                else:
                    at, step = ACQ_LOC * 128 + part * 8 + c, 16
                v.append(lines_ref[pl.ds(at, 16, stride=step), :].astype(jnp.bfloat16))
            for bit in (1, 2, 4):
                clear = (group & bit) == 0
                for i in range(8):
                    if i & bit:
                        continue
                    a, b = v[i], v[i + bit]
                    v[i] = jnp.where(clear, a, pltpu.roll(b, 16 * bit, 1))
                    v[i + bit] = jnp.where(clear, pltpu.roll(a, 128 - 16 * bit, 1), b)
            for o in range(8):
                store(o, part, block, v[o])


def gram(win_ref, mask_ref, o, store):
    row = lax.broadcasted_iota(jnp.int32, (128, 128), 0)
    col = lax.broadcasted_iota(jnp.int32, (128, 128), 1)
    diagonal = row == col
    spare = row % 16 == 15
    dims = (((1,), (1,)), ((), ()))
    for q in range(8):
        re = jnp.concatenate([win_ref[o, 0, q], win_ref[o, 0, q + 1]], axis=1)
        im = jnp.concatenate([win_ref[o, 1, q], win_ref[o, 1, q + 1]], axis=1)
        mask = jnp.concatenate([mask_ref[o, 2 * q : 2 * q + 1, :], mask_ref[o, 2 * q + 1 : 2 * q + 2, :]], axis=1)
        left = jnp.concatenate([re * mask, im * mask], axis=1)
        real = lax.dot_general(left, jnp.concatenate([re, im], axis=1), dims, preferred_element_type=jnp.float32)
        imag = lax.dot_general(left, jnp.concatenate([-im, re], axis=1), dims, preferred_element_type=jnp.float32)
        only = jnp.where(diagonal, real, 0.0)
        power_n = jnp.sum(only, axis=0, keepdims=True)
        power_m = jnp.sum(only, axis=1, keepdims=True)
        scale_n = jnp.where(power_n > 0, lax.rsqrt(power_n), 0.0) * CODE
        scale_m = jnp.where(power_m > 0, lax.rsqrt(power_m), 0.0)
        high = power_n.astype(jnp.bfloat16).astype(jnp.float32)
        code_real = jnp.where(spare, high, jnp.exp2(real * scale_m * scale_n))
        code_imag = jnp.where(spare, power_n - high, jnp.exp2(imag * scale_m * scale_n))
        store(q, code_real.astype(jnp.bfloat16).reshape(8, 16, 128), code_imag.astype(jnp.bfloat16).reshape(8, 16, 128))


def stack_kernel(
    raw_hbm, ramp_ref, mask_ref, out_ref,
    raw_ref, packed_ref, slots_ref, rows_ref, edges_ref, before_ref, after_ref, lines_ref, win_ref, code_ref,
    raw_sem, send_sem, recv_sem, own_sem, edge_send, edge_recv, code_send, code_recv, code_own,
):
    acq, strip = lax.axis_index("acq"), lax.axis_index("strip")
    place = (acq, strip)
    mesh_id = pl.DeviceIdType.MESH

    def device(to):
        return {"acq": to[0], "strip": to[1]}

    barrier = pltpu.get_barrier_semaphore()

    def greet(i, carry):
        pl.semaphore_signal(
            barrier, inc=1, device_id=device(shift(place, i % N_STRIP, i // N_STRIP)), device_id_type=mesh_id
        )
        return carry

    lax.fori_loop(1, N_STRIP * N_GROUP, greet, 0)

    def fetch(s):
        return pltpu.make_async_copy(raw_hbm.at[s], raw_ref.at[s], raw_sem.at[s])

    def fetch_start(i, carry):
        fetch(shift(place, strip_step(i), 0)[1]).start()
        return carry

    lax.fori_loop(0, N_STRIP, fetch_start, 0)
    pl.semaphore_wait(barrier, N_STRIP * N_GROUP - 1)

    own = pltpu.make_async_copy(packed_ref.at[acq, strip], slots_ref.at[acq, strip], own_sem)

    def slot_copy(n, i):
        to = shift(place, strip_step(i), acq_step(n))
        return pltpu.make_async_remote_copy(
            src_ref=packed_ref.at[to[0], to[1]],
            dst_ref=slots_ref.at[acq, strip],
            send_sem=send_sem.at[n * N_STRIP + i],
            recv_sem=recv_sem.at[n * N_STRIP + i],
            device_id=device(to),
            device_id_type=mesh_id,
        )

    def send(n, i):
        @pl.when(n * N_STRIP + i > 0)
        def _():
            slot_copy(n, i).start()

    y = acq // 2

    def early(i, carry):
        s = shift(place, strip_step(i), 0)[1]
        fetch(s).wait()
        pack_tile(raw_ref, ramp_ref, packed_ref, s, y)
        pack_tile(raw_ref, ramp_ref, packed_ref, s, (y + 2) % 4)

        @pl.when(i == 0)
        def _():
            own.start()

        for n in range(4):
            send(n, i)
        return carry

    lax.fori_loop(0, N_STRIP, early, 0)

    def late(i, carry):
        s = shift(place, strip_step(i), 0)[1]
        pack_tile(raw_ref, ramp_ref, packed_ref, s, (y + 1) % 4)
        pack_tile(raw_ref, ramp_ref, packed_ref, s, (y + 3) % 4)
        return carry

    lax.fori_loop(0, N_STRIP, late, 0)

    def late_send(j, carry):
        send(4 + j // N_STRIP, j % N_STRIP)
        return carry

    lax.fori_loop(0, 4 * N_STRIP, late_send, 0)

    def source(n):
        return shift(place, 0, acq_back(acq_step(n)))[0]

    def edge_copy(n, up):
        a = source(n)
        to = (strip + (1 if up else N_STRIP - 1)) % N_STRIP
        return pltpu.make_async_remote_copy(
            src_ref=edges_ref.at[a],
            dst_ref=(before_ref if up else after_ref).at[a],
            send_sem=edge_send.at[1 if up else 0, n],
            recv_sem=edge_recv.at[1 if up else 0, n],
            device_id=device((acq, to)),
            device_id_type=mesh_id,
        )

    has_before = jnp.where(strip > 0, 1.0, 0.0)
    has_after = jnp.where(strip < N_STRIP - 1, 1.0, 0.0)

    def block(n, carry):
        @pl.when(n < N_GROUP)
        def _():
            a = source(n)

            @pl.when(n == 0)
            def _():
                own.wait()

            def arrive(i, carry):
                @pl.when(n * N_STRIP + i > 0)
                def _():
                    slot_copy(n, i).wait_recv()

                return carry

            lax.fori_loop(0, N_STRIP, arrive, 0)
            slots = slots_ref[a].astype(jnp.float32).reshape(N_STRIP * CAP, PIECE).astype(jnp.bfloat16)
            rows_ref[n % 2] = slots
            edges_ref[a] = edge_rows(slots)
            edge_copy(n, True).start()
            edge_copy(n, False).start()

        @pl.when(n > 0)
        def _():
            edge_copy(n - 1, True).wait_recv()
            edge_copy(n - 1, False).wait_recv()
            a = source(n - 1)
            at = pl.ds(pl.multiple_of(a * 16, 16), 16)

            def store(o, part, cols, value):
                win_ref[o, part, cols, at, :] = value

            regroup(
                rows_ref[(n + 1) % 2], before_ref[a], after_ref[a], has_before, has_after, lines_ref, store
            )

        return carry

    lax.fori_loop(0, N_GROUP + 1, block, 0)

    def code_copy(n, o):
        to = shift(place, 0, acq_step(n))
        return pltpu.make_async_remote_copy(
            src_ref=code_ref.at[o, to[0]],
            dst_ref=out_ref.at[acq, o],
            send_sem=code_send.at[n, o],
            recv_sem=code_recv.at[n, o],
            device_id=device(to),
            device_id_type=mesh_id,
        )

    def code_keep(o):
        return pltpu.make_async_copy(code_ref.at[o, acq], out_ref.at[acq, o], code_own.at[o])

    def line(o, carry):
        def store(q, code_real, code_imag):
            code_ref[o, :, q, :, 0:128] = code_real
            code_ref[o, :, q, :, 128:256] = code_imag

        gram(win_ref, mask_ref, o, store)
        for n in range(1, N_GROUP):
            code_copy(n, o).start()
        code_keep(o).start()
        return carry

    lax.fori_loop(0, 8, line, 0)

    def finish(o, carry):
        code_keep(o).wait()
        for n in range(1, N_GROUP):
            code_copy(n, o).wait()
        return carry

    lax.fori_loop(0, 8, finish, 0)

    def sent(j, carry):
        slot_copy(j // N_STRIP, j % N_STRIP).wait_send()
        return carry

    lax.fori_loop(1, N_GROUP * N_STRIP, sent, 0)

    def edge_sent(n, carry):
        edge_copy(n, True).wait_send()
        edge_copy(n, False).wait_send()
        return carry

    lax.fori_loop(0, N_GROUP, edge_sent, 0)


def place_kernel(code_ref, out_ref, flat_ref, power_ref):
    m = pl.program_id(0)

    @pl.when(m == 0)
    def _():
        for o in range(8):
            for g in range(8):
                at = (o * 64 + g * 8) * 16
                block = code_ref[g, o * 8 : o * 8 + 8].astype(jnp.float32)
                block = block.reshape(128, 256)
                flat_ref[0, at : at + 128, :] = block[:, :128]
                flat_ref[1, at : at + 128, :] = block[:, 128:]
        high = flat_ref[0, pl.ds(15, 512, stride=16), :]
        rest = flat_ref[1, pl.ds(15, 512, stride=16), :]
        power_ref[...] = (high + rest).T

    power_n = power_ref[...]
    me = lax.axis_index("acq") * 16 + m
    power_m = power_ref[pl.ds(me, 1), :]
    scale = jnp.sqrt(power_n) * jnp.sqrt(power_m) * lax.rsqrt(power_n * power_m + epsilon)
    for part in range(2):
        codes = flat_ref[part, pl.ds(m, 512, stride=16), :].T
        scaled = jnp.log2(codes) * (1.0 / CODE) * scale
        for block in range(8):
            for t in range(4):
                piece = scaled[block * 16 : block * 16 + ACQ_LOC, t * 128 : t * 128 + 128]
                out_ref[0, pl.ds(block * ACQ_LOC * 8 + t * 2 + part, ACQ_LOC, stride=8), :] = piece


def per_device(
    raw_echo_values,
    cell_target_line,
    cell_track_displacement,
    along_track_chirp_slope,
    along_track_look_radius,
    range_look_radius,
):
    f32, bf16 = jnp.float32, jnp.bfloat16
    squared = cell_track_displacement[0].astype(f32) ** 2
    phase = squared[..., None] * along_track_chirp_slope
    line = cell_target_line[0].astype(f32)[..., None]
    gap = jnp.zeros((N_STRIP, CAP, 64 - ACQ_LOC), f32)
    ramp = jnp.concatenate([jnp.cos(phase), gap, jnp.sin(phase), gap[..., 1:], line], axis=-1)
    raw = raw_echo_values.reshape(N_STRIP, CAP, ACQ_LOC, 2, 4, 128)
    raw = raw.transpose(0, 1, 2, 4, 3, 5).reshape(N_STRIP, CAP * ACQ_LOC * 8, 128)
    group = lax.axis_index("acq")
    radius = lax.dynamic_slice_in_dim(range_look_radius, group * 8, 8, 0)
    across = jnp.arange(16, dtype=jnp.int32)[None, :] - 8
    col_mask = (jnp.abs(across) <= radius[:, None]).reshape(8, 2, 8)
    row_mask = jnp.abs(across) <= along_track_look_radius[:, None]
    masks = (row_mask[:, None, None, None, :] & col_mask[None, :, :, :, None]).reshape(8, 16, 128).astype(bf16)
    dma = pltpu.SemaphoreType.DMA
    received = pl.pallas_call(
        stack_kernel,
        out_shape=jax.ShapeDtypeStruct((N_GROUP, 8, 8, 16, 256), bf16),
        in_specs=[
            pl.BlockSpec(memory_space=pl.ANY),
            pl.BlockSpec(memory_space=pltpu.VMEM),
            pl.BlockSpec(memory_space=pltpu.VMEM),
        ],
        out_specs=pl.BlockSpec(memory_space=pl.ANY),
        scratch_shapes=[
            pltpu.VMEM((N_STRIP, CAP * ACQ_LOC * 8, 128), f32),
            pltpu.VMEM((N_GROUP, N_STRIP, CAP, PIECE), bf16),
            pltpu.VMEM((N_GROUP, N_STRIP, CAP, PIECE), bf16),
            pltpu.VMEM((2, N_STRIP * CAP, PIECE), bf16),
            pltpu.VMEM((N_GROUP, 16, PIECE), bf16),
            pltpu.VMEM((N_GROUP, 16, PIECE), bf16),
            pltpu.VMEM((N_GROUP, 16, PIECE), bf16),
            pltpu.VMEM((PIECE, 128), f32),
            pltpu.VMEM((8, 2, 9, 128, 128), bf16),
            pltpu.VMEM((8, N_GROUP, 8, 16, 256), bf16),
            dma((N_STRIP,)),
            dma((N_GROUP * N_STRIP,)),
            dma((N_GROUP * N_STRIP,)),
            dma,
            dma((2, N_GROUP)),
            dma((2, N_GROUP)),
            dma((N_GROUP, 8)),
            dma((N_GROUP, 8)),
            dma((8,)),
        ],
        compiler_params=pltpu.CompilerParams(vmem_limit_bytes=VMEM, collective_id=0, has_side_effects=True),
        name="stack",
    )(raw, ramp, masks)
    received = received.reshape(N_GROUP, 64, 16, 256)
    placed = pl.pallas_call(
        place_kernel,
        grid=(ACQ_LOC,),
        out_shape=jax.ShapeDtypeStruct((ACQ_LOC, 960, 128), f32),
        in_specs=[pl.BlockSpec((8, 64, 16, 256), lambda m: (0, 0, 0, 0))],
        out_specs=pl.BlockSpec((1, 960, 128), lambda m: (m, 0, 0)),
        scratch_shapes=[pltpu.VMEM((2, 512 * 16, 128), f32), pltpu.VMEM((128, 512), f32)],
        compiler_params=params(),
        name="place",
    )(received)
    placed = placed.reshape(ACQ_LOC, 120, 4, 2, 128).transpose(0, 1, 3, 2, 4)
    return placed.reshape(ACQ_LOC, 120, 2, 512)


def solution(mesh):
    placed = (
        P("strip", None, None, "acq", None, None),
        P("strip", None, None),
        P("strip", None, None),
        P("acq"),
        P("strip"),
        P(),
    )
    return jax.shard_map(
        per_device,
        mesh=mesh,
        in_specs=placed,
        out_specs=P("acq", None, None, "strip"),
        check_vma=False,
    )
```

```python
import jax
import jax.numpy as jnp
from jax import lax
from jax.experimental import pallas as pl
from jax.experimental.pallas import tpu as pltpu
from jax.sharding import PartitionSpec as P

epsilon = 1e-06
N_STRIP = 16
N_GROUP = 8
CAP = 8
ACQ_LOC = 15
PIECE = 2176
ROW_LANE = 2168
PLACE = 3
CODE = 120.0
VMEM = 56 * 1024 * 1024


def params(limit=VMEM):
    return pltpu.CompilerParams(vmem_limit_bytes=limit)


def shift(place, strip_step, acq_step):
    acq, strip = place
    dx, dz, dc = (strip_step // 2) % 4, strip_step // 8, strip_step % 2
    dy, dh = acq_step // 2, acq_step % 2
    to_strip = ((strip // 8 + dz) % 2) * 8 + (((strip // 2) % 4 + dx) % 4) * 2 + (strip % 2 + dc) % 2
    to_acq = ((acq // 2 + dy) % 4) * 2 + (acq % 2 + dh) % 2
    return to_acq, to_strip


def strip_step(i):
    return (i * 11) % N_STRIP


def back(step):
    return (step // 8) * 8 + ((4 - (step // 2) % 4) % 4) * 2 + step % 2


def acq_step(n):
    half, rest = n // 4, n % 4
    dy = (1 - half) * (rest // 2) * 2 + half * (1 + 2 * (rest % 2))
    dh = (1 - half) * (rest % 2) + half * (rest // 2)
    return dy * 2 + dh


def acq_back(step):
    return ((4 - step // 2) % 4) * 2 + step % 2


def pack_strip(raw_ref, packed_ref, s, line, phase):
    cosines, sines = jnp.cos(phase), jnp.sin(phase)
    lane = lax.broadcasted_iota(jnp.int32, (CAP, 128), 1)
    lane16 = lax.broadcasted_iota(jnp.int32, (2 * CAP, 128), 1)
    low, low16 = lane < 64, lane16 < 64
    halo = [jnp.zeros((2 * CAP, 128), jnp.bfloat16) for _ in range(N_GROUP)]
    for a in range(ACQ_LOC):
        cosine = jnp.broadcast_to(cosines[:, a : a + 1], (CAP, 128))
        sine = jnp.broadcast_to(sines[:, a : a + 1], (CAP, 128))
        tiles = []
        for t in range(4):
            row = a * 8 + t * 2
            real = raw_ref[s, pl.ds(row, CAP, stride=ACQ_LOC * 8), :]
            imag = raw_ref[s, pl.ds(row + 1, CAP, stride=ACQ_LOC * 8), :]
            new_real = real * cosine + imag * sine
            new_imag = imag * cosine - real * sine
            tiles.append(jnp.concatenate([new_real, new_imag], axis=0).astype(jnp.bfloat16))
            even = jnp.where(low, new_real, pltpu.roll(new_imag, 64, 1))
            odd = jnp.where(low, pltpu.roll(new_real, 64, 1), new_imag)
            packed_ref[2 * t, s, :, a * 128 : a * 128 + 128] = even.astype(jnp.bfloat16)
            packed_ref[2 * t + 1, s, :, a * 128 : a * 128 + 128] = odd.astype(jnp.bfloat16)
        left = (lane16 >= a * 8) & (lane16 < a * 8 + 4)
        right = (lane16 >= a * 8 + 4) & (lane16 < a * 8 + 8)
        for bound in range(1, N_GROUP):
            t = bound // 2
            if bound % 2:
                source, start = tiles[t], 60
            else:
                source, start = jnp.where(low16, tiles[t], tiles[t - 1]), 124
            moved = pltpu.roll(source, (a * 8 - start) % 128, 1)
            halo[bound] = jnp.where(left, moved, halo[bound])
            halo[bound - 1] = jnp.where(right, moved, halo[bound - 1])
    for group in range(N_GROUP):
        both = halo[group].astype(jnp.float32)
        for part in range(2):
            at = ACQ_LOC * 128 + part * 128
            rows = both[part * CAP : part * CAP + CAP]
            if part:
                rows = jnp.where(lane == ROW_LANE - at, line, rows)
            packed_ref[group, s, :, at : at + 128] = rows.astype(jnp.bfloat16)


def edge_rows(slots):
    line = slots[:, ROW_LANE : ROW_LANE + 1].astype(jnp.float32)
    index = lax.broadcasted_iota(jnp.int32, (128, 16), 1)
    wanted = jnp.where(index < 4, index, jnp.where(index < 8, index + 56, 1000)).astype(jnp.float32)
    pick = (line == wanted).astype(jnp.float32).astype(jnp.bfloat16)
    dims = (((0,), (0,)), ((), ()))
    total = lax.dot_general(pick, slots, dims, preferred_element_type=jnp.float32)
    count = lax.dot_general(pick, jnp.ones((128, 128), jnp.bfloat16), dims, preferred_element_type=jnp.float32)
    inverse = 1.0 / jnp.maximum(count[:, :1], 1.0)
    return (total * inverse).astype(jnp.bfloat16)


def regroup(slots, before, after, has_before, has_after, lines_ref, store):
    line = slots[:, ROW_LANE : ROW_LANE + 1].astype(jnp.float32)
    lane = lax.broadcasted_iota(jnp.int32, (128, 128), 1)
    row = 8 * (lane // 16) + lane % 16 - 4
    inside = (row >= 0) & (row < 64)
    pick = (line == jnp.where(inside, row, 1000).astype(jnp.float32)).astype(jnp.float32)
    lane16 = lax.broadcasted_iota(jnp.int32, (16, 128), 1)
    sub16 = lax.broadcasted_iota(jnp.int32, (16, 128), 0)
    pick_before = ((lane16 < 4) & (sub16 == lane16 + 4)).astype(jnp.float32) * has_before
    pick_after = ((lane16 >= 124) & (sub16 == lane16 - 124)).astype(jnp.float32) * has_after
    picks = jnp.concatenate([pick, pick_before, pick_after], axis=0)
    inverse = 1.0 / jnp.maximum(jnp.sum(picks, axis=0, keepdims=True), 1.0)
    rows = jnp.concatenate([slots, before, after], axis=0)
    total = lax.dot_general(
        rows, picks.astype(jnp.bfloat16), (((0,), (0,)), ((), ())), preferred_element_type=jnp.float32
    )
    lines_ref[...] = total * inverse
    group = lane16 // 16
    for part in range(2):
        for block in range(9):
            v = []
            for c in range(8):
                col = 8 * block + c - 4
                if 0 <= col < 64:
                    at, step = part * 64 + col, 128
                else:
                    at, step = ACQ_LOC * 128 + part * 128 + c, 8
                v.append(lines_ref[pl.ds(at, 16, stride=step), :].astype(jnp.bfloat16))
            v = [pltpu.roll(v[i], 16 * i, 1) if i else v[i] for i in range(8)]
            v = [v[-i % 8] for i in range(8)]
            for bit in (1, 2, 4):
                moving = (group & bit) != 0
                v = [jnp.where(moving, v[(i - bit) % 8], v[i]) for i in range(8)]
            v = [pltpu.roll(v[i], 128 - 16 * i, 1) if i else v[i] for i in range(8)]
            for o in range(8):
                store(o, part, block, v[o])


def gram(win_ref, row_radius, col_radius, o, store):
    row = lax.broadcasted_iota(jnp.int32, (128, 128), 0)
    col = lax.broadcasted_iota(jnp.int32, (128, 128), 1)
    diagonal = row == col
    spare = row % 16 == 15
    dims = (((1,), (1,)), ((), ()))
    lane = lax.broadcasted_iota(jnp.int32, (1, 256), 1)
    row_mask = (jnp.abs(lane % 16 - 8) <= row_radius).astype(jnp.float32)
    for q in range(8):
        re = jnp.concatenate([win_ref[o, 0, q], win_ref[o, 0, q + 1]], axis=1)
        im = jnp.concatenate([win_ref[o, 1, q], win_ref[o, 1, q + 1]], axis=1)
        mask = (jnp.abs(lane // 16 - 8) <= col_radius(q)).astype(jnp.float32)
        mask = (mask * row_mask).astype(jnp.bfloat16)
        left = jnp.concatenate([re * mask, im * mask], axis=1)
        real = lax.dot_general(left, jnp.concatenate([re, im], axis=1), dims, preferred_element_type=jnp.float32)
        imag = lax.dot_general(left, jnp.concatenate([-im, re], axis=1), dims, preferred_element_type=jnp.float32)
        only = jnp.where(diagonal, real, 0.0)
        power_n = jnp.sum(only, axis=0, keepdims=True)
        power_m = jnp.sum(only, axis=1, keepdims=True)
        scale_n = jnp.where(power_n > 0, lax.rsqrt(power_n), 0.0) * CODE
        scale_m = jnp.where(power_m > 0, lax.rsqrt(power_m), 0.0)
        high = power_n.astype(jnp.bfloat16).astype(jnp.float32)
        code_real = jnp.where(spare, high, jnp.exp2(real * scale_m * scale_n))
        code_imag = jnp.where(spare, power_n - high, jnp.exp2(imag * scale_m * scale_n))
        store(q, code_real.astype(jnp.bfloat16).reshape(8, 16, 128), code_imag.astype(jnp.bfloat16).reshape(8, 16, 128))


def stack_kernel(
    raw_hbm, line_ref, offset_ref, slope_ref, row_radius_ref, col_radius_ref, out_ref,
    raw_ref, packed_ref, slots_ref, rows_ref, edges_ref, before_ref, after_ref, lines_ref, win_ref, code_ref,
    raw_sem, send_sem, recv_sem, own_sem, edge_send, edge_recv, code_send, code_recv, code_own,
):
    acq, strip = lax.axis_index("acq"), lax.axis_index("strip")
    place = (acq, strip)
    mesh_id = pl.DeviceIdType.MESH

    def device(to):
        return {"acq": to[0], "strip": to[1]}

    barrier = pltpu.get_barrier_semaphore()

    def greet(i, carry):
        pl.semaphore_signal(
            barrier, inc=1, device_id=device(shift(place, i % N_STRIP, i // N_STRIP)), device_id_type=mesh_id
        )
        return carry

    lax.fori_loop(1, N_STRIP * N_GROUP, greet, 0)

    def fetch(s):
        return pltpu.make_async_copy(raw_hbm.at[s], raw_ref.at[s], raw_sem.at[s])

    def fetch_start(i, carry):
        fetch(shift(place, strip_step(i), 0)[1]).start()
        return carry

    lax.fori_loop(0, N_STRIP, fetch_start, 0)
    squared = offset_ref[...].astype(jnp.float32) ** 2
    lines = line_ref[...].astype(jnp.float32)
    reader_lane = lax.broadcasted_iota(jnp.int32, (CAP, N_STRIP), 1)

    def pack(i, carry):
        s = shift(place, strip_step(i), 0)[1]
        fetch(s).wait()
        mine = reader_lane == s
        column = jnp.sum(jnp.where(mine, squared, 0.0), axis=1, keepdims=True)
        line = jnp.sum(jnp.where(mine, lines, 0.0), axis=1, keepdims=True)
        pack_strip(raw_ref, packed_ref, s, line, column * slope_ref[...])
        return carry

    lax.fori_loop(0, N_STRIP, pack, 0)
    pl.semaphore_wait(barrier, N_STRIP * N_GROUP - 1)

    own = pltpu.make_async_copy(packed_ref.at[acq, strip], slots_ref.at[acq, strip], own_sem)

    def slot_copy(n, i):
        to = shift(place, strip_step(i), acq_step(n))
        return pltpu.make_async_remote_copy(
            src_ref=packed_ref.at[to[0], to[1]],
            dst_ref=slots_ref.at[acq, strip],
            send_sem=send_sem.at[n * N_STRIP + i],
            recv_sem=recv_sem.at[n * N_STRIP + i],
            device_id=device(to),
            device_id_type=mesh_id,
        )

    def send(n, i):
        @pl.when(n * N_STRIP + i > 0)
        def _():
            slot_copy(n, i).start()

    own.start()
    for some in ((0, 1, 2, 3), (4, 5), (6, 7)):

        def send_some(i, carry):
            for n in some:
                send(n, i)
            return carry

        lax.fori_loop(0, N_STRIP, send_some, 0)

    def source(n):
        return shift(place, 0, acq_back(acq_step(n)))[0]

    def edge_copy(n, up):
        a = source(n)
        to = (strip + (1 if up else N_STRIP - 1)) % N_STRIP
        return pltpu.make_async_remote_copy(
            src_ref=edges_ref.at[a],
            dst_ref=(before_ref if up else after_ref).at[a],
            send_sem=edge_send.at[1 if up else 0, n],
            recv_sem=edge_recv.at[1 if up else 0, n],
            device_id=device((acq, to)),
            device_id_type=mesh_id,
        )

    has_before = jnp.where(strip > 0, 1.0, 0.0)
    has_after = jnp.where(strip < N_STRIP - 1, 1.0, 0.0)

    def block(n, carry):
        @pl.when(n < N_GROUP)
        def _():
            a = source(n)

            @pl.when(n == 0)
            def _():
                own.wait()

            def arrive(i, carry):
                @pl.when(n * N_STRIP + i > 0)
                def _():
                    slot_copy(n, i).wait_recv()

                return carry

            lax.fori_loop(0, N_STRIP, arrive, 0)
            slots = slots_ref[a].astype(jnp.float32).reshape(N_STRIP * CAP, PIECE).astype(jnp.bfloat16)
            rows_ref[n % 2] = slots
            edges_ref[a] = edge_rows(slots)
            edge_copy(n, True).start()
            edge_copy(n, False).start()

        @pl.when(n > 0)
        def _():
            edge_copy(n - 1, True).wait_recv()
            edge_copy(n - 1, False).wait_recv()
            a = source(n - 1)
            at = pl.ds(pl.multiple_of(a * 16, 16), 16)

            def store(o, part, cols, value):
                win_ref[o, part, cols, at, :] = value

            regroup(
                rows_ref[(n + 1) % 2], before_ref[a], after_ref[a], has_before, has_after, lines_ref, store
            )

        return carry

    lax.fori_loop(0, N_GROUP + 1, block, 0)

    def code_copy(n, o):
        to = shift(place, 0, acq_step(n))
        return pltpu.make_async_remote_copy(
            src_ref=code_ref.at[o, to[0]],
            dst_ref=out_ref.at[acq, o],
            send_sem=code_send.at[n, o],
            recv_sem=code_recv.at[n, o],
            device_id=device(to),
            device_id_type=mesh_id,
        )

    def code_keep(o):
        return pltpu.make_async_copy(code_ref.at[o, acq], out_ref.at[acq, o], code_own.at[o])

    def line(o, carry):
        def store(q, code_real, code_imag):
            code_ref[o, :, q, :, 0:128] = code_real
            code_ref[o, :, q, :, 128:256] = code_imag

        gram(win_ref, row_radius_ref[o], lambda q: col_radius_ref[acq * 8 + q], o, store)
        for n in range(1, N_GROUP):
            code_copy(n, o).start()
        code_keep(o).start()
        return carry

    lax.fori_loop(0, 8, line, 0)

    def finish(o, carry):
        code_keep(o).wait()
        for n in range(1, N_GROUP):
            code_copy(n, o).wait()
        return carry

    lax.fori_loop(0, 8, finish, 0)

    def sent(j, carry):
        slot_copy(j // N_STRIP, j % N_STRIP).wait_send()
        return carry

    lax.fori_loop(1, N_GROUP * N_STRIP, sent, 0)

    def edge_sent(n, carry):
        edge_copy(n, True).wait_send()
        edge_copy(n, False).wait_send()
        return carry

    lax.fori_loop(0, N_GROUP, edge_sent, 0)


def place_kernel(code_ref, out_ref, flat_ref, power_ref):
    step = pl.program_id(0)

    @pl.when(step == 0)
    def _():
        for o in range(8):
            for g in range(8):
                at = (o * 64 + g * 8) * 16
                block = code_ref[g, o * 8 : o * 8 + 8].astype(jnp.float32)
                block = block.reshape(128, 256)
                flat_ref[0, at : at + 128, :] = block[:, :128]
                flat_ref[1, at : at + 128, :] = block[:, 128:]
        high = flat_ref[0, pl.ds(15, 512, stride=16), :]
        rest = flat_ref[1, pl.ds(15, 512, stride=16), :]
        power_ref[...] = (high + rest).T

    power_n = power_ref[...]
    root_n = jnp.sqrt(power_n)
    for j in range(PLACE):
        m = step * PLACE + j
        me = lax.axis_index("acq") * 16 + m
        power_m = power_ref[pl.ds(me, 1), :]
        scale = root_n * jnp.sqrt(power_m) * lax.rsqrt(power_n * power_m + epsilon) * (1.0 / CODE)
        for part in range(2):
            codes = flat_ref[part, pl.ds(m, 512, stride=16), :].T
            scaled = jnp.log2(codes) * scale
            for block in range(8):
                for t in range(4):
                    piece = scaled[block * 16 : block * 16 + ACQ_LOC, t * 128 : t * 128 + 128]
                    out_ref[j, pl.ds(block * ACQ_LOC * 8 + t * 2 + part, ACQ_LOC, stride=8), :] = piece


def per_device(
    raw_echo_values,
    cell_target_line,
    cell_track_displacement,
    along_track_chirp_slope,
    along_track_look_radius,
    range_look_radius,
):
    f32, bf16 = jnp.float32, jnp.bfloat16
    raw = raw_echo_values.reshape(N_STRIP, CAP, ACQ_LOC, 2, 4, 128)
    raw = raw.transpose(0, 1, 2, 4, 3, 5).reshape(N_STRIP, CAP * ACQ_LOC * 8, 128)
    dma = pltpu.SemaphoreType.DMA
    received = pl.pallas_call(
        stack_kernel,
        out_shape=jax.ShapeDtypeStruct((N_GROUP, 8, 8, 16, 256), bf16),
        in_specs=[
            pl.BlockSpec(memory_space=pl.ANY),
            pl.BlockSpec(memory_space=pltpu.VMEM),
            pl.BlockSpec(memory_space=pltpu.VMEM),
            pl.BlockSpec(memory_space=pltpu.VMEM),
            pl.BlockSpec(memory_space=pltpu.SMEM),
            pl.BlockSpec(memory_space=pltpu.SMEM),
        ],
        out_specs=pl.BlockSpec(memory_space=pl.ANY),
        scratch_shapes=[
            pltpu.VMEM((N_STRIP, CAP * ACQ_LOC * 8, 128), f32),
            pltpu.VMEM((N_GROUP, N_STRIP, CAP, PIECE), bf16),
            pltpu.VMEM((N_GROUP, N_STRIP, CAP, PIECE), bf16),
            pltpu.VMEM((2, N_STRIP * CAP, PIECE), bf16),
            pltpu.VMEM((N_GROUP, 16, PIECE), bf16),
            pltpu.VMEM((N_GROUP, 16, PIECE), bf16),
            pltpu.VMEM((N_GROUP, 16, PIECE), bf16),
            pltpu.VMEM((PIECE, 128), f32),
            pltpu.VMEM((8, 2, 9, 128, 128), bf16),
            pltpu.VMEM((8, N_GROUP, 8, 16, 256), bf16),
            dma((N_STRIP,)),
            dma((N_GROUP * N_STRIP,)),
            dma((N_GROUP * N_STRIP,)),
            dma,
            dma((2, N_GROUP)),
            dma((2, N_GROUP)),
            dma((N_GROUP, 8)),
            dma((N_GROUP, 8)),
            dma((8,)),
        ],
        compiler_params=pltpu.CompilerParams(vmem_limit_bytes=VMEM, collective_id=0, has_side_effects=True),
        name="stack",
    )(
        raw,
        cell_target_line[0].T,
        cell_track_displacement[0].T,
        along_track_chirp_slope[None],
        along_track_look_radius,
        range_look_radius,
    )
    received = received.reshape(N_GROUP, 64, 16, 256)
    placed = pl.pallas_call(
        place_kernel,
        grid=(ACQ_LOC // PLACE,),
        out_shape=jax.ShapeDtypeStruct((ACQ_LOC, 960, 128), f32),
        in_specs=[pl.BlockSpec((8, 64, 16, 256), lambda m: (0, 0, 0, 0))],
        out_specs=pl.BlockSpec((PLACE, 960, 128), lambda m: (m, 0, 0)),
        scratch_shapes=[pltpu.VMEM((2, 512 * 16, 128), f32), pltpu.VMEM((128, 512), f32)],
        compiler_params=params(),
        name="place",
    )(received)
    placed = placed.reshape(ACQ_LOC, 120, 4, 2, 128).transpose(0, 1, 3, 2, 4)
    return placed.reshape(ACQ_LOC, 120, 2, 512)


def solution(mesh):
    placed = (
        P("strip", None, None, "acq", None, None),
        P("strip", None, None),
        P("strip", None, None),
        P("acq"),
        P("strip"),
        P(),
    )
    return jax.shard_map(
        per_device,
        mesh=mesh,
        in_specs=placed,
        out_specs=P("acq", None, None, "strip"),
        check_vma=False,
    )
```

```python
import jax
import jax.numpy as jnp
from jax import lax
from jax.experimental import pallas as pl
from jax.experimental.pallas import tpu as pltpu
from jax.sharding import PartitionSpec as P

epsilon = 1e-06
N_STRIP = 16
N_GROUP = 8
CAP = 8
ACQ_LOC = 15
PIECE = 2176
ROW_LANE = 2168
EARLY = 8
PLACE = 3
CODE = 120.0
VMEM = 56 * 1024 * 1024


def params(limit=VMEM):
    return pltpu.CompilerParams(vmem_limit_bytes=limit)


def shift(place, strip_step, acq_step):
    acq, strip = place
    dx, dz, dc = (strip_step // 2) % 4, strip_step // 8, strip_step % 2
    dy, dh = acq_step // 2, acq_step % 2
    to_strip = ((strip // 8 + dz) % 2) * 8 + (((strip // 2) % 4 + dx) % 4) * 2 + (strip % 2 + dc) % 2
    to_acq = ((acq // 2 + dy) % 4) * 2 + (acq % 2 + dh) % 2
    return to_acq, to_strip


def strip_step(i):
    return (i * 11) % N_STRIP


def back(step):
    return (step // 8) * 8 + ((4 - (step // 2) % 4) % 4) * 2 + step % 2


def acq_step(n):
    far, second, odd = n // 4, (n // 2) % 2, n % 2
    dy = far + 2 * ((second + odd) % 2)
    dh = (second + odd) % 2 + (1 - 2 * ((second + odd) % 2)) * second
    return dy * 2 + dh


def acq_back(step):
    return ((4 - step // 2) % 4) * 2 + step % 2


def pack_strip(raw_ref, packed_ref, s, line, phase):
    cosines, sines = jnp.cos(phase), jnp.sin(phase)
    lane = lax.broadcasted_iota(jnp.int32, (CAP, 128), 1)
    lane16 = lax.broadcasted_iota(jnp.int32, (2 * CAP, 128), 1)
    low, low16 = lane < 64, lane16 < 64
    halo = [jnp.zeros((2 * CAP, 128), jnp.bfloat16) for _ in range(N_GROUP)]
    for a in range(ACQ_LOC):
        cosine = jnp.broadcast_to(cosines[:, a : a + 1], (CAP, 128))
        sine = jnp.broadcast_to(sines[:, a : a + 1], (CAP, 128))
        tiles = []
        for t in range(4):
            row = a * 8 + t * 2
            real = raw_ref[s, pl.ds(row, CAP, stride=ACQ_LOC * 8), :]
            imag = raw_ref[s, pl.ds(row + 1, CAP, stride=ACQ_LOC * 8), :]
            new_real = real * cosine + imag * sine
            new_imag = imag * cosine - real * sine
            tiles.append(jnp.concatenate([new_real, new_imag], axis=0).astype(jnp.bfloat16))
            even = jnp.where(low, new_real, pltpu.roll(new_imag, 64, 1))
            odd = jnp.where(low, pltpu.roll(new_real, 64, 1), new_imag)
            packed_ref[2 * t, s, :, a * 128 : a * 128 + 128] = even.astype(jnp.bfloat16)
            packed_ref[2 * t + 1, s, :, a * 128 : a * 128 + 128] = odd.astype(jnp.bfloat16)
        left = (lane16 >= a * 8) & (lane16 < a * 8 + 4)
        right = (lane16 >= a * 8 + 4) & (lane16 < a * 8 + 8)
        for bound in range(1, N_GROUP):
            t = bound // 2
            if bound % 2:
                source, start = tiles[t], 60
            else:
                source, start = jnp.where(low16, tiles[t], tiles[t - 1]), 124
            moved = pltpu.roll(source, (a * 8 - start) % 128, 1)
            halo[bound] = jnp.where(left, moved, halo[bound])
            halo[bound - 1] = jnp.where(right, moved, halo[bound - 1])
    for group in range(N_GROUP):
        both = halo[group].astype(jnp.float32)
        for part in range(2):
            at = ACQ_LOC * 128 + part * 128
            rows = both[part * CAP : part * CAP + CAP]
            if part:
                rows = jnp.where(lane == ROW_LANE - at, line, rows)
            packed_ref[group, s, :, at : at + 128] = rows.astype(jnp.bfloat16)


def edge_rows(slots):
    line = slots[:, ROW_LANE : ROW_LANE + 1].astype(jnp.float32)
    index = lax.broadcasted_iota(jnp.int32, (128, 16), 1)
    wanted = jnp.where(index < 4, index, jnp.where(index < 8, index + 56, 1000)).astype(jnp.float32)
    pick = (line == wanted).astype(jnp.float32).astype(jnp.bfloat16)
    dims = (((0,), (0,)), ((), ()))
    total = lax.dot_general(pick, slots, dims, preferred_element_type=jnp.float32)
    count = lax.dot_general(pick, jnp.ones((128, 128), jnp.bfloat16), dims, preferred_element_type=jnp.float32)
    inverse = 1.0 / jnp.maximum(count[:, :1], 1.0)
    return (total * inverse).astype(jnp.bfloat16)


def window_picks(slots):
    line = slots[:, ROW_LANE : ROW_LANE + 1].astype(jnp.float32)
    lane = lax.broadcasted_iota(jnp.int32, (128, 128), 1)
    row = 8 * (lane // 16) + lane % 16 - 4
    inside = (row >= 0) & (row < 64)
    return (line == jnp.where(inside, row, 1000).astype(jnp.float32)).astype(jnp.float32)


def border_picks(has_before, has_after):
    lane = lax.broadcasted_iota(jnp.int32, (32, 128), 1)
    sub = lax.broadcasted_iota(jnp.int32, (32, 128), 0)
    before = ((lane < 4) & (sub == lane + 4)).astype(jnp.float32) * has_before
    after = ((lane >= 124) & (sub == lane - 108)).astype(jnp.float32) * has_after
    return before + after


def regroup(rows, picks, lines_ref, store):
    inverse = 1.0 / jnp.maximum(jnp.sum(picks, axis=0, keepdims=True), 1.0)
    total = lax.dot_general(
        rows, picks.astype(jnp.bfloat16), (((0,), (0,)), ((), ())), preferred_element_type=jnp.float32
    )
    lines_ref[...] = total * inverse
    group = lax.broadcasted_iota(jnp.int32, (16, 128), 1) // 16
    for part in range(2):
        for block in range(9):
            v = []
            for c in range(8):
                col = 8 * block + c - 4
                if 0 <= col < 64:
                    at, step = part * 64 + col, 128
                else:
                    at, step = ACQ_LOC * 128 + part * 128 + c, 8
                v.append(lines_ref[pl.ds(at, 16, stride=step), :].astype(jnp.bfloat16))
            v = [pltpu.roll(v[i], 16 * i, 1) if i else v[i] for i in range(8)]
            v = [v[-i % 8] for i in range(8)]
            for bit in (1, 2, 4):
                moving = (group & bit) != 0
                v = [jnp.where(moving, v[(i - bit) % 8], v[i]) for i in range(8)]
            store(part, block, v)


def turned(value, o):
    return pltpu.roll(value, 128 - 16 * o, 1) if o else value


def gram(win_ref, row_radius, col_radius, o, store):
    row = lax.broadcasted_iota(jnp.int32, (128, 128), 0)
    col = lax.broadcasted_iota(jnp.int32, (128, 128), 1)
    diagonal = row == col
    spare = row % 16 == 15
    dims = (((1,), (1,)), ((), ()))
    lane = lax.broadcasted_iota(jnp.int32, (1, 256), 1)
    row_mask = (jnp.abs(lane % 16 - 8) <= row_radius).astype(jnp.float32)
    for q in range(8):
        re = jnp.concatenate([win_ref[o, 0, q], win_ref[o, 0, q + 1]], axis=1)
        im = jnp.concatenate([win_ref[o, 1, q], win_ref[o, 1, q + 1]], axis=1)
        mask = (jnp.abs(lane // 16 - 8) <= col_radius(q)).astype(jnp.float32)
        mask = (mask * row_mask).astype(jnp.bfloat16)
        left = jnp.concatenate([re * mask, im * mask], axis=1)
        real = lax.dot_general(left, jnp.concatenate([re, im], axis=1), dims, preferred_element_type=jnp.float32)
        imag = lax.dot_general(left, jnp.concatenate([-im, re], axis=1), dims, preferred_element_type=jnp.float32)
        only = jnp.where(diagonal, real, 0.0)
        power_n = jnp.sum(only, axis=0, keepdims=True)
        power_m = jnp.sum(only, axis=1, keepdims=True)
        scale_n = jnp.where(power_n > 0, lax.rsqrt(power_n), 0.0) * CODE
        scale_m = jnp.where(power_m > 0, lax.rsqrt(power_m), 0.0)
        high = power_n.astype(jnp.bfloat16).astype(jnp.float32)
        code_real = jnp.where(spare, high, jnp.exp2(real * scale_m * scale_n))
        code_imag = jnp.where(spare, power_n - high, jnp.exp2(imag * scale_m * scale_n))
        store(q, code_real.astype(jnp.bfloat16).reshape(8, 16, 128), code_imag.astype(jnp.bfloat16).reshape(8, 16, 128))


def stack_kernel(
    raw_hbm, line_ref, offset_ref, slope_ref, row_radius_ref, col_radius_ref, out_ref,
    raw_ref, packed_ref, slots_ref, edges_ref, before_ref, after_ref, lines_ref, win_ref, code_ref,
    group_sem, raw_sem, send_sem, recv_sem, own_sem, edge_send, edge_recv, code_send, code_recv, code_own,
):
    acq, strip = lax.axis_index("acq"), lax.axis_index("strip")
    place = (acq, strip)
    mesh_id = pl.DeviceIdType.MESH

    def device(to):
        return {"acq": to[0], "strip": to[1]}

    barrier = pltpu.get_barrier_semaphore()

    def greet(semaphore, to):
        pl.semaphore_signal(semaphore, inc=1, device_id=device(to), device_id_type=mesh_id)

    for i in range(1, N_STRIP):
        greet(barrier, shift(place, i, 0))
    for n in range(1, N_GROUP):
        greet(barrier, shift(place, 0, n))

    def fetch(s):
        return pltpu.make_async_copy(raw_hbm.at[s], raw_ref.at[s], raw_sem.at[s])

    def fetch_start(i, carry):
        fetch(shift(place, strip_step(i), 0)[1]).start()
        return carry

    lax.fori_loop(0, N_STRIP, fetch_start, 0)
    squared = offset_ref[...].astype(jnp.float32) ** 2
    lines = line_ref[...].astype(jnp.float32)
    reader_lane = lax.broadcasted_iota(jnp.int32, (CAP, N_STRIP), 1)

    def pack(i, carry):
        s = shift(place, strip_step(i), 0)[1]
        fetch(s).wait()
        mine = reader_lane == s
        column = jnp.sum(jnp.where(mine, squared, 0.0), axis=1, keepdims=True)
        line = jnp.sum(jnp.where(mine, lines, 0.0), axis=1, keepdims=True)
        pack_strip(raw_ref, packed_ref, s, line, column * slope_ref[...])
        return carry

    lax.fori_loop(0, 2, pack, 0)
    pl.semaphore_wait(barrier, N_STRIP + N_GROUP - 2)
    for n in range(1, N_GROUP):
        greet(group_sem, shift(place, 0, n))
    lax.fori_loop(2, EARLY, pack, 0)
    pl.semaphore_wait(group_sem, N_GROUP - 1)

    own = pltpu.make_async_copy(packed_ref.at[acq, strip], slots_ref.at[acq, strip], own_sem)

    def slot_copy(n, i):
        to = shift(place, strip_step(i), acq_step(n))
        return pltpu.make_async_remote_copy(
            src_ref=packed_ref.at[to[0], to[1]],
            dst_ref=slots_ref.at[acq, strip],
            send_sem=send_sem.at[n * N_STRIP + i],
            recv_sem=recv_sem.at[n * N_STRIP + i],
            device_id=device(to),
            device_id_type=mesh_id,
        )

    def send(n, i):
        @pl.when(n * N_STRIP + i > 0)
        def _():
            slot_copy(n, i).start()

    def send_pair(first):
        def body(i, carry):
            send(first, i)
            send(first + 1, i)
            return carry

        return body

    def pack_and_send(i, carry):
        pack(i, carry)
        return send_pair(0)(i, carry)

    lax.fori_loop(0, EARLY, send_pair(0), 0)
    lax.fori_loop(EARLY, N_STRIP, pack_and_send, 0)
    own.start()
    for first in (2, 4, 6):
        lax.fori_loop(0, N_STRIP, send_pair(first), 0)

    def source(n):
        return shift(place, 0, acq_back(acq_step(n)))[0]

    def edge_copy(up):
        to = (strip + (1 if up else N_STRIP - 1)) % N_STRIP
        return pltpu.make_async_remote_copy(
            src_ref=edges_ref,
            dst_ref=before_ref if up else after_ref,
            send_sem=edge_send.at[1 if up else 0],
            recv_sem=edge_recv.at[1 if up else 0],
            device_id=device((acq, to)),
            device_id_type=mesh_id,
        )

    def rows_of(a):
        return pl.ds(pl.multiple_of(a * 16, 16), 16)

    def block(n, carry):
        a = source(n)

        @pl.when(n == 0)
        def _():
            own.wait()

        def arrive(i, carry):
            @pl.when(n * N_STRIP + i > 0)
            def _():
                slot_copy(n, i).wait_recv()

            return carry

        lax.fori_loop(0, N_STRIP, arrive, 0)
        slots = slots_ref[a].astype(jnp.float32).reshape(N_STRIP * CAP, PIECE).astype(jnp.bfloat16)
        edges_ref[a] = edge_rows(slots)

        def store(part, cols, value):
            for o in range(8):
                win_ref[o, part, cols, rows_of(a), :] = turned(value[o], o)

        regroup(slots, window_picks(slots), lines_ref, store)
        return carry

    lax.fori_loop(0, N_GROUP, block, 0)
    edge_copy(True).start()
    edge_copy(False).start()

    def code_copy(n, o):
        to = shift(place, 0, acq_step(n))
        return pltpu.make_async_remote_copy(
            src_ref=code_ref.at[o, to[0]],
            dst_ref=out_ref.at[acq, o],
            send_sem=code_send.at[n, o],
            recv_sem=code_recv.at[n, o],
            device_id=device(to),
            device_id_type=mesh_id,
        )

    def code_keep(o):
        return pltpu.make_async_copy(code_ref.at[o, acq], out_ref.at[acq, o], code_own.at[o])

    def line(o, carry):
        def store(q, code_real, code_imag):
            code_ref[o, :, q, :, 0:128] = code_real
            code_ref[o, :, q, :, 128:256] = code_imag

        gram(win_ref, row_radius_ref[o], lambda q: col_radius_ref[acq * 8 + q], o, store)
        for n in range(1, N_GROUP):
            code_copy(n, o).start()
        code_keep(o).start()
        return carry

    lax.fori_loop(1, 7, line, 0)

    edge_copy(True).wait_recv()
    edge_copy(False).wait_recv()
    picks = border_picks(jnp.where(strip > 0, 1.0, 0.0), jnp.where(strip < N_STRIP - 1, 1.0, 0.0))

    def border(a, carry):
        def store(part, cols, value):
            for o in (0, 7):
                win_ref[o, part, cols, rows_of(a), :] += turned(value[o], o)

        regroup(jnp.concatenate([before_ref[a], after_ref[a]], axis=0), picks, lines_ref, store)
        return carry

    lax.fori_loop(0, N_GROUP, border, 0)
    line(0, 0)
    line(7, 0)

    def finish(o, carry):
        code_keep(o).wait()
        for n in range(1, N_GROUP):
            code_copy(n, o).wait()
        return carry

    lax.fori_loop(0, 8, finish, 0)

    def sent(j, carry):
        slot_copy(j // N_STRIP, j % N_STRIP).wait_send()
        return carry

    lax.fori_loop(1, N_GROUP * N_STRIP, sent, 0)

    edge_copy(True).wait_send()
    edge_copy(False).wait_send()


def place_kernel(code_ref, out_ref, flat_ref, power_ref):
    step = pl.program_id(0)

    @pl.when(step == 0)
    def _():
        for o in range(8):
            for g in range(8):
                at = (o * 64 + g * 8) * 16
                block = code_ref[g, o * 8 : o * 8 + 8].astype(jnp.float32)
                block = block.reshape(128, 256)
                flat_ref[0, at : at + 128, :] = block[:, :128]
                flat_ref[1, at : at + 128, :] = block[:, 128:]
        high = flat_ref[0, pl.ds(15, 512, stride=16), :]
        rest = flat_ref[1, pl.ds(15, 512, stride=16), :]
        power_ref[...] = (high + rest).T

    power_n = power_ref[...]
    root_n = jnp.sqrt(power_n)
    for j in range(PLACE):
        m = step * PLACE + j
        me = lax.axis_index("acq") * 16 + m
        power_m = power_ref[pl.ds(me, 1), :]
        scale = root_n * jnp.sqrt(power_m) * lax.rsqrt(power_n * power_m + epsilon) * (1.0 / CODE)
        for part in range(2):
            codes = flat_ref[part, pl.ds(m, 512, stride=16), :].T
            scaled = jnp.log2(codes) * scale
            for block in range(8):
                for t in range(4):
                    piece = scaled[block * 16 : block * 16 + ACQ_LOC, t * 128 : t * 128 + 128]
                    out_ref[j, pl.ds(block * ACQ_LOC * 8 + t * 2 + part, ACQ_LOC, stride=8), :] = piece


def per_device(
    raw_echo_values,
    cell_target_line,
    cell_track_displacement,
    along_track_chirp_slope,
    along_track_look_radius,
    range_look_radius,
):
    f32, bf16 = jnp.float32, jnp.bfloat16
    raw = raw_echo_values.reshape(N_STRIP, CAP, ACQ_LOC, 2, 4, 128)
    raw = raw.transpose(0, 1, 2, 4, 3, 5).reshape(N_STRIP, CAP * ACQ_LOC * 8, 128)
    dma = pltpu.SemaphoreType.DMA
    received = pl.pallas_call(
        stack_kernel,
        out_shape=jax.ShapeDtypeStruct((N_GROUP, 8, 8, 16, 256), bf16),
        in_specs=[
            pl.BlockSpec(memory_space=pl.ANY),
            pl.BlockSpec(memory_space=pltpu.VMEM),
            pl.BlockSpec(memory_space=pltpu.VMEM),
            pl.BlockSpec(memory_space=pltpu.VMEM),
            pl.BlockSpec(memory_space=pltpu.SMEM),
            pl.BlockSpec(memory_space=pltpu.SMEM),
        ],
        out_specs=pl.BlockSpec(memory_space=pl.ANY),
        scratch_shapes=[
            pltpu.VMEM((N_STRIP, CAP * ACQ_LOC * 8, 128), f32),
            pltpu.VMEM((N_GROUP, N_STRIP, CAP, PIECE), bf16),
            pltpu.VMEM((N_GROUP, N_STRIP, CAP, PIECE), bf16),
            pltpu.VMEM((N_GROUP, 16, PIECE), bf16),
            pltpu.VMEM((N_GROUP, 16, PIECE), bf16),
            pltpu.VMEM((N_GROUP, 16, PIECE), bf16),
            pltpu.VMEM((PIECE, 128), f32),
            pltpu.VMEM((8, 2, 9, 128, 128), bf16),
            pltpu.VMEM((8, N_GROUP, 8, 16, 256), bf16),
            pltpu.SemaphoreType.REGULAR,
            dma((N_STRIP,)),
            dma((N_GROUP * N_STRIP,)),
            dma((N_GROUP * N_STRIP,)),
            dma,
            dma((2,)),
            dma((2,)),
            dma((N_GROUP, 8)),
            dma((N_GROUP, 8)),
            dma((8,)),
        ],
        compiler_params=pltpu.CompilerParams(vmem_limit_bytes=VMEM, collective_id=0, has_side_effects=True),
        name="stack",
    )(
        raw,
        cell_target_line[0].T,
        cell_track_displacement[0].T,
        along_track_chirp_slope[None],
        along_track_look_radius,
        range_look_radius,
    )
    received = received.reshape(N_GROUP, 64, 16, 256)
    placed = pl.pallas_call(
        place_kernel,
        grid=(ACQ_LOC // PLACE,),
        out_shape=jax.ShapeDtypeStruct((ACQ_LOC, 960, 128), f32),
        in_specs=[pl.BlockSpec((8, 64, 16, 256), lambda m: (0, 0, 0, 0))],
        out_specs=pl.BlockSpec((PLACE, 960, 128), lambda m: (m, 0, 0)),
        scratch_shapes=[pltpu.VMEM((2, 512 * 16, 128), f32), pltpu.VMEM((128, 512), f32)],
        compiler_params=params(),
        name="place",
    )(received)
    placed = placed.reshape(ACQ_LOC, 120, 4, 2, 128).transpose(0, 1, 3, 2, 4)
    return placed.reshape(ACQ_LOC, 120, 2, 512)


def solution(mesh):
    placed = (
        P("strip", None, None, "acq", None, None),
        P("strip", None, None),
        P("strip", None, None),
        P("acq"),
        P("strip"),
        P(),
    )
    return jax.shard_map(
        per_device,
        mesh=mesh,
        in_specs=placed,
        out_specs=P("acq", None, None, "strip"),
        check_vma=False,
    )
```

```python
import jax
import jax.numpy as jnp
from jax import lax
from jax.experimental import pallas as pl
from jax.experimental.pallas import tpu as pltpu
from jax.sharding import PartitionSpec as P

epsilon = 1e-06
N_STRIP = 16
N_GROUP = 8
CAP = 8
ACQ_LOC = 15
PIECE = 2176
ROW_LANE = 2168
EARLY = 2
PLACE = 3
CODE = 120.0
VMEM = 56 * 1024 * 1024


def params(limit=VMEM):
    return pltpu.CompilerParams(vmem_limit_bytes=limit)


def shift(place, strip_step, acq_step):
    acq, strip = place
    dx, dz, dc = (strip_step // 2) % 4, strip_step // 8, strip_step % 2
    dy, dh = acq_step // 2, acq_step % 2
    to_strip = ((strip // 8 + dz) % 2) * 8 + (((strip // 2) % 4 + dx) % 4) * 2 + (strip % 2 + dc) % 2
    to_acq = ((acq // 2 + dy) % 4) * 2 + (acq % 2 + dh) % 2
    return to_acq, to_strip


def strip_step(i):
    return (i * 11) % N_STRIP


def back(step):
    return (step // 8) * 8 + ((4 - (step // 2) % 4) % 4) * 2 + step % 2


def acq_step(n):
    far, second, odd = n // 4, (n // 2) % 2, n % 2
    dy = far + 2 * ((second + odd) % 2)
    dh = (second + odd) % 2 + (1 - 2 * ((second + odd) % 2)) * second
    return dy * 2 + dh


def acq_back(step):
    return ((4 - step // 2) % 4) * 2 + step % 2


def pack_strip(raw_ref, packed_ref, s, line, phase):
    cosines, sines = jnp.cos(phase), jnp.sin(phase)
    lane = lax.broadcasted_iota(jnp.int32, (CAP, 128), 1)
    lane16 = lax.broadcasted_iota(jnp.int32, (2 * CAP, 128), 1)
    low, low16 = lane < 64, lane16 < 64
    halo = [jnp.zeros((2 * CAP, 128), jnp.bfloat16) for _ in range(N_GROUP)]
    for a in range(ACQ_LOC):
        cosine = jnp.broadcast_to(cosines[:, a : a + 1], (CAP, 128))
        sine = jnp.broadcast_to(sines[:, a : a + 1], (CAP, 128))
        tiles = []
        for t in range(4):
            row = a * 8 + t * 2
            real = raw_ref[s, pl.ds(row, CAP, stride=ACQ_LOC * 8), :]
            imag = raw_ref[s, pl.ds(row + 1, CAP, stride=ACQ_LOC * 8), :]
            new_real = real * cosine + imag * sine
            new_imag = imag * cosine - real * sine
            tiles.append(jnp.concatenate([new_real, new_imag], axis=0).astype(jnp.bfloat16))
            even = jnp.where(low, new_real, pltpu.roll(new_imag, 64, 1))
            odd = jnp.where(low, pltpu.roll(new_real, 64, 1), new_imag)
            packed_ref[2 * t, s, :, a * 128 : a * 128 + 128] = even.astype(jnp.bfloat16)
            packed_ref[2 * t + 1, s, :, a * 128 : a * 128 + 128] = odd.astype(jnp.bfloat16)
        left = (lane16 >= a * 8) & (lane16 < a * 8 + 4)
        right = (lane16 >= a * 8 + 4) & (lane16 < a * 8 + 8)
        for bound in range(1, N_GROUP):
            t = bound // 2
            if bound % 2:
                source, start = tiles[t], 60
            else:
                source, start = jnp.where(low16, tiles[t], tiles[t - 1]), 124
            moved = pltpu.roll(source, (a * 8 - start) % 128, 1)
            halo[bound] = jnp.where(left, moved, halo[bound])
            halo[bound - 1] = jnp.where(right, moved, halo[bound - 1])
    for group in range(N_GROUP):
        both = halo[group].astype(jnp.float32)
        for part in range(2):
            at = ACQ_LOC * 128 + part * 128
            rows = both[part * CAP : part * CAP + CAP]
            if part:
                rows = jnp.where(lane == ROW_LANE - at, line, rows)
            packed_ref[group, s, :, at : at + 128] = rows.astype(jnp.bfloat16)


def edge_rows(slots):
    line = slots[:, ROW_LANE : ROW_LANE + 1].astype(jnp.float32)
    index = lax.broadcasted_iota(jnp.int32, (128, 16), 1)
    wanted = jnp.where(index < 4, index, jnp.where(index < 8, index + 56, 1000)).astype(jnp.float32)
    pick = (line == wanted).astype(jnp.float32).astype(jnp.bfloat16)
    dims = (((0,), (0,)), ((), ()))
    total = lax.dot_general(pick, slots, dims, preferred_element_type=jnp.float32)
    count = lax.dot_general(pick, jnp.ones((128, 128), jnp.bfloat16), dims, preferred_element_type=jnp.float32)
    inverse = 1.0 / jnp.maximum(count[:, :1], 1.0)
    return (total * inverse).astype(jnp.bfloat16)


def window_picks(slots):
    line = slots[:, ROW_LANE : ROW_LANE + 1].astype(jnp.float32)
    lane = lax.broadcasted_iota(jnp.int32, (128, 128), 1)
    row = 8 * (lane // 16) + lane % 16 - 4
    inside = (row >= 0) & (row < 64)
    return (line == jnp.where(inside, row, 1000).astype(jnp.float32)).astype(jnp.float32)


def border_picks(has_before, has_after):
    lane = lax.broadcasted_iota(jnp.int32, (32, 128), 1)
    sub = lax.broadcasted_iota(jnp.int32, (32, 128), 0)
    before = ((lane < 4) & (sub == lane + 4)).astype(jnp.float32) * has_before
    after = ((lane >= 124) & (sub == lane - 108)).astype(jnp.float32) * has_after
    return before + after


def regroup(rows, picks, lines_ref, store):
    inverse = 1.0 / jnp.maximum(jnp.sum(picks, axis=0, keepdims=True), 1.0)
    total = lax.dot_general(
        rows, picks.astype(jnp.bfloat16), (((0,), (0,)), ((), ())), preferred_element_type=jnp.float32
    )
    lines_ref[...] = total * inverse
    group = lax.broadcasted_iota(jnp.int32, (16, 128), 1) // 16
    for part in range(2):
        for block in range(9):
            v = []
            for c in range(8):
                col = 8 * block + c - 4
                if 0 <= col < 64:
                    at, step = part * 64 + col, 128
                else:
                    at, step = ACQ_LOC * 128 + part * 128 + c, 8
                v.append(lines_ref[pl.ds(at, 16, stride=step), :].astype(jnp.bfloat16))
            v = [pltpu.roll(v[i], 16 * i, 1) if i else v[i] for i in range(8)]
            v = [v[-i % 8] for i in range(8)]
            for bit in (1, 2, 4):
                moving = (group & bit) != 0
                v = [jnp.where(moving, v[(i - bit) % 8], v[i]) for i in range(8)]
            store(part, block, v)


def turned(value, o):
    return pltpu.roll(value, 128 - 16 * o, 1) if o else value


def gram(win_ref, row_radius, col_radius, o, store):
    row = lax.broadcasted_iota(jnp.int32, (128, 128), 0)
    col = lax.broadcasted_iota(jnp.int32, (128, 128), 1)
    diagonal = row == col
    spare = row % 16 == 15
    dims = (((1,), (1,)), ((), ()))
    lane = lax.broadcasted_iota(jnp.int32, (1, 256), 1)
    row_mask = (jnp.abs(lane % 16 - 8) <= row_radius).astype(jnp.float32)
    for q in range(8):
        re = jnp.concatenate([win_ref[o, 0, q], win_ref[o, 0, q + 1]], axis=1)
        im = jnp.concatenate([win_ref[o, 1, q], win_ref[o, 1, q + 1]], axis=1)
        mask = (jnp.abs(lane // 16 - 8) <= col_radius(q)).astype(jnp.float32)
        mask = (mask * row_mask).astype(jnp.bfloat16)
        left = jnp.concatenate([re * mask, im * mask], axis=1)
        real = lax.dot_general(left, jnp.concatenate([re, im], axis=1), dims, preferred_element_type=jnp.float32)
        imag = lax.dot_general(left, jnp.concatenate([-im, re], axis=1), dims, preferred_element_type=jnp.float32)
        only = jnp.where(diagonal, real, 0.0)
        power_n = jnp.sum(only, axis=0, keepdims=True)
        power_m = jnp.sum(only, axis=1, keepdims=True)
        scale_n = jnp.where(power_n > 0, lax.rsqrt(power_n), 0.0) * CODE
        scale_m = jnp.where(power_m > 0, lax.rsqrt(power_m), 0.0)
        high = power_n.astype(jnp.bfloat16).astype(jnp.float32)
        code_real = jnp.where(spare, high, jnp.exp2(real * scale_m * scale_n))
        code_imag = jnp.where(spare, power_n - high, jnp.exp2(imag * scale_m * scale_n))
        store(q, code_real.astype(jnp.bfloat16).reshape(8, 16, 128), code_imag.astype(jnp.bfloat16).reshape(8, 16, 128))


def stack_kernel(
    raw_hbm, line_ref, offset_ref, slope_ref, row_radius_ref, col_radius_ref, out_ref,
    raw_ref, packed_ref, slots_ref, edges_ref, before_ref, after_ref, lines_ref, win_ref, code_ref,
    group_sem, raw_sem, send_sem, recv_sem, own_sem, edge_send, edge_recv, code_send, code_recv, code_own,
):
    acq, strip = lax.axis_index("acq"), lax.axis_index("strip")
    place = (acq, strip)
    mesh_id = pl.DeviceIdType.MESH

    def device(to):
        return {"acq": to[0], "strip": to[1]}

    barrier = pltpu.get_barrier_semaphore()

    def greet(semaphore, to):
        pl.semaphore_signal(semaphore, inc=1, device_id=device(to), device_id_type=mesh_id)

    for i in range(1, N_STRIP):
        greet(barrier, shift(place, i, 0))
    for n in range(1, N_GROUP):
        greet(barrier, shift(place, 0, n))

    def fetch(s):
        return pltpu.make_async_copy(raw_hbm.at[s], raw_ref.at[s], raw_sem.at[s])

    def fetch_start(i, carry):
        fetch(shift(place, strip_step(i), 0)[1]).start()
        return carry

    lax.fori_loop(0, N_STRIP, fetch_start, 0)
    squared = offset_ref[...].astype(jnp.float32) ** 2
    lines = line_ref[...].astype(jnp.float32)
    reader_lane = lax.broadcasted_iota(jnp.int32, (CAP, N_STRIP), 1)

    def pack(i, carry):
        s = shift(place, strip_step(i), 0)[1]
        fetch(s).wait()
        mine = reader_lane == s
        column = jnp.sum(jnp.where(mine, squared, 0.0), axis=1, keepdims=True)
        line = jnp.sum(jnp.where(mine, lines, 0.0), axis=1, keepdims=True)
        pack_strip(raw_ref, packed_ref, s, line, column * slope_ref[...])
        return carry

    lax.fori_loop(0, 2, pack, 0)
    pl.semaphore_wait(barrier, N_STRIP + N_GROUP - 2)
    for n in range(1, N_GROUP):
        greet(group_sem, shift(place, 0, n))
    lax.fori_loop(2, EARLY, pack, 0)
    pl.semaphore_wait(group_sem, N_GROUP - 1)

    own = pltpu.make_async_copy(packed_ref.at[acq, strip], slots_ref.at[acq, strip], own_sem)

    def slot_copy(n, i):
        to = shift(place, strip_step(i), acq_step(n))
        return pltpu.make_async_remote_copy(
            src_ref=packed_ref.at[to[0], to[1]],
            dst_ref=slots_ref.at[acq, strip],
            send_sem=send_sem.at[n * N_STRIP + i],
            recv_sem=recv_sem.at[n],
            device_id=device(to),
            device_id_type=mesh_id,
        )

    def send(n, i):
        @pl.when(n * N_STRIP + i > 0)
        def _():
            slot_copy(n, i).start()

    def send_pair(first):
        def body(i, carry):
            send(first, i)
            send(first + 1, i)
            return carry

        return body

    def pack_and_send(i, carry):
        pack(i, carry)
        return send_pair(0)(i, carry)

    lax.fori_loop(0, EARLY, send_pair(0), 0)
    lax.fori_loop(EARLY, N_STRIP, pack_and_send, 0)
    own.start()
    for first in (2, 4, 6):
        lax.fori_loop(0, N_STRIP, send_pair(first), 0)

    def source(n):
        return shift(place, 0, acq_back(acq_step(n)))[0]

    def edge_copy(up):
        to = (strip + (1 if up else N_STRIP - 1)) % N_STRIP
        return pltpu.make_async_remote_copy(
            src_ref=edges_ref,
            dst_ref=before_ref if up else after_ref,
            send_sem=edge_send.at[1 if up else 0],
            recv_sem=edge_recv.at[1 if up else 0],
            device_id=device((acq, to)),
            device_id_type=mesh_id,
        )

    def rows_of(a):
        return pl.ds(pl.multiple_of(a * 16, 16), 16)

    def arrival(n, a, count):
        return pltpu.make_async_remote_copy(
            src_ref=packed_ref.at[a, pl.ds(0, count)],
            dst_ref=slots_ref.at[a, pl.ds(0, count)],
            send_sem=send_sem.at[n],
            recv_sem=recv_sem.at[n],
            device_id=device((acq, (strip + 1) % N_STRIP)),
            device_id_type=mesh_id,
        )

    def slots_of(a):
        return slots_ref[a].astype(jnp.float32).reshape(N_STRIP * CAP, PIECE).astype(jnp.bfloat16)

    def block(n, carry):
        a = source(n)

        @pl.when(n == 0)
        def _():
            own.wait()
            arrival(n, a, N_STRIP - 1).wait_recv()

        @pl.when(n > 0)
        def _():
            arrival(n, a, N_STRIP).wait_recv()

        slots = slots_of(a)

        def store(part, cols, value):
            for o in range(8):
                win_ref[o, part, cols, rows_of(a), :] = turned(value[o], o)

        regroup(slots, window_picks(slots), lines_ref, store)
        return carry

    lax.fori_loop(0, N_GROUP, block, 0)

    def code_copy(n, o):
        to = shift(place, 0, acq_step(n))
        return pltpu.make_async_remote_copy(
            src_ref=code_ref.at[o, to[0]],
            dst_ref=out_ref.at[acq, o],
            send_sem=code_send.at[n, o],
            recv_sem=code_recv.at[n, o],
            device_id=device(to),
            device_id_type=mesh_id,
        )

    def code_keep(o):
        return pltpu.make_async_copy(code_ref.at[o, acq], out_ref.at[acq, o], code_own.at[o])

    def line(o, carry):
        def store(q, code_real, code_imag):
            code_ref[o, :, q, :, 0:128] = code_real
            code_ref[o, :, q, :, 128:256] = code_imag

        gram(win_ref, row_radius_ref[o], lambda q: col_radius_ref[acq * 8 + q], o, store)
        for n in range(1, N_GROUP):
            code_copy(n, o).start()
        code_keep(o).start()
        return carry

    line(1, 0)

    def edge(a, carry):
        edges_ref[a] = edge_rows(slots_of(a))
        return carry

    lax.fori_loop(0, N_GROUP, edge, 0)
    edge_copy(True).start()
    edge_copy(False).start()
    lax.fori_loop(2, 7, line, 0)

    edge_copy(True).wait_recv()
    edge_copy(False).wait_recv()
    picks = border_picks(jnp.where(strip > 0, 1.0, 0.0), jnp.where(strip < N_STRIP - 1, 1.0, 0.0))

    def border(a, carry):
        def store(part, cols, value):
            for o in (0, 7):
                win_ref[o, part, cols, rows_of(a), :] += turned(value[o], o)

        regroup(jnp.concatenate([before_ref[a], after_ref[a]], axis=0), picks, lines_ref, store)
        return carry

    lax.fori_loop(0, N_GROUP, border, 0)
    line(0, 0)
    line(7, 0)

    def sent(j, carry):
        slot_copy(j // N_STRIP, j % N_STRIP).wait_send()
        return carry

    lax.fori_loop(1, N_GROUP * N_STRIP, sent, 0)
    edge_copy(True).wait_send()
    edge_copy(False).wait_send()

    def finish(j, carry):
        o = (j + 1) % 7 + 6 * (j // 7)
        code_keep(o).wait()
        for n in range(1, N_GROUP):
            code_copy(n, o).wait()
        return carry

    lax.fori_loop(0, 8, finish, 0)


def place_kernel(code_ref, out_ref, flat_ref, power_ref):
    step = pl.program_id(0)

    @pl.when(step == 0)
    def _():
        for o in range(8):
            for g in range(8):
                at = (o * 64 + g * 8) * 16
                block = code_ref[g, o * 8 : o * 8 + 8].astype(jnp.float32)
                block = block.reshape(128, 256)
                flat_ref[0, at : at + 128, :] = block[:, :128]
                flat_ref[1, at : at + 128, :] = block[:, 128:]
        high = flat_ref[0, pl.ds(15, 512, stride=16), :]
        rest = flat_ref[1, pl.ds(15, 512, stride=16), :]
        power_ref[...] = (high + rest).T

    power_n = power_ref[...]
    root_n = jnp.sqrt(power_n)
    for j in range(PLACE):
        m = step * PLACE + j
        me = lax.axis_index("acq") * 16 + m
        power_m = power_ref[pl.ds(me, 1), :]
        scale = root_n * jnp.sqrt(power_m) * lax.rsqrt(power_n * power_m + epsilon) * (1.0 / CODE)
        for part in range(2):
            codes = flat_ref[part, pl.ds(m, 512, stride=16), :].T
            scaled = jnp.log2(codes) * scale
            for block in range(8):
                for t in range(4):
                    piece = scaled[block * 16 : block * 16 + ACQ_LOC, t * 128 : t * 128 + 128]
                    out_ref[j, pl.ds(block * ACQ_LOC * 8 + t * 2 + part, ACQ_LOC, stride=8), :] = piece


def per_device(
    raw_echo_values,
    cell_target_line,
    cell_track_displacement,
    along_track_chirp_slope,
    along_track_look_radius,
    range_look_radius,
):
    f32, bf16 = jnp.float32, jnp.bfloat16
    raw = raw_echo_values.reshape(N_STRIP, CAP, ACQ_LOC, 2, 4, 128)
    raw = raw.transpose(0, 1, 2, 4, 3, 5).reshape(N_STRIP, CAP * ACQ_LOC * 8, 128)
    dma = pltpu.SemaphoreType.DMA
    received = pl.pallas_call(
        stack_kernel,
        out_shape=jax.ShapeDtypeStruct((N_GROUP, 8, 8, 16, 256), bf16),
        in_specs=[
            pl.BlockSpec(memory_space=pl.ANY),
            pl.BlockSpec(memory_space=pltpu.VMEM),
            pl.BlockSpec(memory_space=pltpu.VMEM),
            pl.BlockSpec(memory_space=pltpu.VMEM),
            pl.BlockSpec(memory_space=pltpu.SMEM),
            pl.BlockSpec(memory_space=pltpu.SMEM),
        ],
        out_specs=pl.BlockSpec(memory_space=pl.ANY),
        scratch_shapes=[
            pltpu.VMEM((N_STRIP, CAP * ACQ_LOC * 8, 128), f32),
            pltpu.VMEM((N_GROUP, N_STRIP, CAP, PIECE), bf16),
            pltpu.VMEM((N_GROUP, N_STRIP, CAP, PIECE), bf16),
            pltpu.VMEM((N_GROUP, 16, PIECE), bf16),
            pltpu.VMEM((N_GROUP, 16, PIECE), bf16),
            pltpu.VMEM((N_GROUP, 16, PIECE), bf16),
            pltpu.VMEM((PIECE, 128), f32),
            pltpu.VMEM((8, 2, 9, 128, 128), bf16),
            pltpu.VMEM((8, N_GROUP, 8, 16, 256), bf16),
            pltpu.SemaphoreType.REGULAR,
            dma((N_STRIP,)),
            dma((N_GROUP * N_STRIP,)),
            dma((N_GROUP,)),
            dma,
            dma((2,)),
            dma((2,)),
            dma((N_GROUP, 8)),
            dma((N_GROUP, 8)),
            dma((8,)),
        ],
        compiler_params=pltpu.CompilerParams(vmem_limit_bytes=VMEM, collective_id=0, has_side_effects=True),
        name="stack",
    )(
        raw,
        cell_target_line[0].T,
        cell_track_displacement[0].T,
        along_track_chirp_slope[None],
        along_track_look_radius,
        range_look_radius,
    )
    received = received.reshape(N_GROUP, 64, 16, 256)
    placed = pl.pallas_call(
        place_kernel,
        grid=(ACQ_LOC // PLACE,),
        out_shape=jax.ShapeDtypeStruct((ACQ_LOC, 960, 128), f32),
        in_specs=[pl.BlockSpec((8, 64, 16, 256), lambda m: (0, 0, 0, 0))],
        out_specs=pl.BlockSpec((PLACE, 960, 128), lambda m: (m, 0, 0)),
        scratch_shapes=[pltpu.VMEM((2, 512 * 16, 128), f32), pltpu.VMEM((128, 512), f32)],
        compiler_params=params(),
        name="place",
    )(received)
    placed = placed.reshape(ACQ_LOC, 120, 4, 2, 128).transpose(0, 1, 3, 2, 4)
    return placed.reshape(ACQ_LOC, 120, 2, 512)


def solution(mesh):
    placed = (
        P("strip", None, None, "acq", None, None),
        P("strip", None, None),
        P("strip", None, None),
        P("acq"),
        P("strip"),
        P(),
    )
    return jax.shard_map(
        per_device,
        mesh=mesh,
        in_specs=placed,
        out_specs=P("acq", None, None, "strip"),
        check_vma=False,
    )
```

```python
import jax
import jax.numpy as jnp
from jax import lax
from jax.experimental import pallas as pl
from jax.experimental.pallas import tpu as pltpu
from jax.sharding import PartitionSpec as P

epsilon = 1e-06
N_STRIP = 16
N_GROUP = 8
CAP = 8
ACQ_LOC = 15
PIECE = 2176
ROW_LANE = 2168
EARLY = 2
PLACE = 3
CODE = 120.0
VMEM = 56 * 1024 * 1024


def params(limit=VMEM):
    return pltpu.CompilerParams(vmem_limit_bytes=limit)


def shift(place, strip_step, acq_step):
    acq, strip = place
    dx, dz, dc = (strip_step // 2) % 4, strip_step // 8, strip_step % 2
    dy, dh = acq_step // 2, acq_step % 2
    to_strip = ((strip // 8 + dz) % 2) * 8 + (((strip // 2) % 4 + dx) % 4) * 2 + (strip % 2 + dc) % 2
    to_acq = ((acq // 2 + dy) % 4) * 2 + (acq % 2 + dh) % 2
    return to_acq, to_strip


def strip_step(i):
    return (i * 11) % N_STRIP


def back(step):
    return (step // 8) * 8 + ((4 - (step // 2) % 4) % 4) * 2 + step % 2


def acq_step(n):
    far, second, odd = n // 4, (n // 2) % 2, n % 2
    dy = far + 2 * ((second + odd) % 2)
    dh = (second + odd) % 2 + (1 - 2 * ((second + odd) % 2)) * second
    return dy * 2 + dh


def acq_back(step):
    return ((4 - step // 2) % 4) * 2 + step % 2


def pack_strip(raw_ref, packed_ref, s, line, phase):
    cosines, sines = jnp.cos(phase), jnp.sin(phase)
    lane = lax.broadcasted_iota(jnp.int32, (CAP, 128), 1)
    lane16 = lax.broadcasted_iota(jnp.int32, (2 * CAP, 128), 1)
    low, low16 = lane < 64, lane16 < 64
    halo = [jnp.zeros((2 * CAP, 128), jnp.bfloat16) for _ in range(N_GROUP)]
    for a in range(ACQ_LOC):
        cosine = jnp.broadcast_to(cosines[:, a : a + 1], (CAP, 128))
        sine = jnp.broadcast_to(sines[:, a : a + 1], (CAP, 128))
        tiles = []
        for t in range(4):
            row = a * 8 + t * 2
            real = raw_ref[s, pl.ds(row, CAP, stride=ACQ_LOC * 8), :]
            imag = raw_ref[s, pl.ds(row + 1, CAP, stride=ACQ_LOC * 8), :]
            new_real = real * cosine + imag * sine
            new_imag = imag * cosine - real * sine
            tiles.append(jnp.concatenate([new_real, new_imag], axis=0).astype(jnp.bfloat16))
            even = jnp.where(low, new_real, pltpu.roll(new_imag, 64, 1))
            odd = jnp.where(low, pltpu.roll(new_real, 64, 1), new_imag)
            packed_ref[2 * t, s, :, a * 128 : a * 128 + 128] = even.astype(jnp.bfloat16)
            packed_ref[2 * t + 1, s, :, a * 128 : a * 128 + 128] = odd.astype(jnp.bfloat16)
        left = (lane16 >= a * 8) & (lane16 < a * 8 + 4)
        right = (lane16 >= a * 8 + 4) & (lane16 < a * 8 + 8)
        for bound in range(1, N_GROUP):
            t = bound // 2
            if bound % 2:
                source, start = tiles[t], 60
            else:
                source, start = jnp.where(low16, tiles[t], tiles[t - 1]), 124
            moved = pltpu.roll(source, (a * 8 - start) % 128, 1)
            halo[bound] = jnp.where(left, moved, halo[bound])
            halo[bound - 1] = jnp.where(right, moved, halo[bound - 1])
    for group in range(N_GROUP):
        both = halo[group].astype(jnp.float32)
        for part in range(2):
            at = ACQ_LOC * 128 + part * 128
            rows = both[part * CAP : part * CAP + CAP]
            if part:
                rows = jnp.where(lane == ROW_LANE - at, line, rows)
            packed_ref[group, s, :, at : at + 128] = rows.astype(jnp.bfloat16)


def edge_rows(slots):
    line = slots[:, ROW_LANE : ROW_LANE + 1].astype(jnp.float32)
    index = lax.broadcasted_iota(jnp.int32, (128, 16), 1)
    wanted = jnp.where(index < 4, index, jnp.where(index < 8, index + 56, 1000)).astype(jnp.float32)
    pick = (line == wanted).astype(jnp.float32).astype(jnp.bfloat16)
    dims = (((0,), (0,)), ((), ()))
    total = lax.dot_general(pick, slots, dims, preferred_element_type=jnp.float32)
    count = lax.dot_general(pick, jnp.ones((128, 128), jnp.bfloat16), dims, preferred_element_type=jnp.float32)
    inverse = 1.0 / jnp.maximum(count[:, :1], 1.0)
    return (total * inverse).astype(jnp.bfloat16)


def window_picks(slots):
    line = slots[:, ROW_LANE : ROW_LANE + 1].astype(jnp.float32)
    lane = lax.broadcasted_iota(jnp.int32, (128, 128), 1)
    row = 8 * (lane // 16) + lane % 16 - 4
    inside = (row >= 0) & (row < 64)
    return (line == jnp.where(inside, row, 1000).astype(jnp.float32)).astype(jnp.float32)


def border_picks(has_before, has_after):
    lane = lax.broadcasted_iota(jnp.int32, (32, 128), 1)
    sub = lax.broadcasted_iota(jnp.int32, (32, 128), 0)
    before = ((lane < 4) & (sub == lane + 4)).astype(jnp.float32) * has_before
    after = ((lane >= 124) & (sub == lane - 108)).astype(jnp.float32) * has_after
    return before + after


def regroup(rows, picks, lines_ref, store):
    inverse = 1.0 / jnp.maximum(jnp.sum(picks, axis=0, keepdims=True), 1.0)
    total = lax.dot_general(
        rows, picks.astype(jnp.bfloat16), (((0,), (0,)), ((), ())), preferred_element_type=jnp.float32
    )
    lines_ref[...] = total * inverse
    group = lax.broadcasted_iota(jnp.int32, (16, 128), 1) // 16
    for part in range(2):
        for block in range(9):
            v = []
            for c in range(8):
                col = 8 * block + c - 4
                if 0 <= col < 64:
                    at, step = part * 64 + col, 128
                else:
                    at, step = ACQ_LOC * 128 + part * 128 + c, 8
                v.append(lines_ref[pl.ds(at, 16, stride=step), :].astype(jnp.bfloat16))
            v = [pltpu.roll(v[i], 16 * i, 1) if i else v[i] for i in range(8)]
            v = [v[-i % 8] for i in range(8)]
            for bit in (1, 2, 4):
                moving = (group & bit) != 0
                v = [jnp.where(moving, v[(i - bit) % 8], v[i]) for i in range(8)]
            store(part, block, v)


def turned(value, o):
    return pltpu.roll(value, 128 - 16 * o, 1) if o else value


def gram(win_ref, row_radius, col_radius, o, store):
    row = lax.broadcasted_iota(jnp.int32, (128, 128), 0)
    col = lax.broadcasted_iota(jnp.int32, (128, 128), 1)
    diagonal = row == col
    spare = row % 16 == 15
    dims = (((1,), (1,)), ((), ()))
    lane = lax.broadcasted_iota(jnp.int32, (1, 256), 1)
    row_mask = (jnp.abs(lane % 16 - 8) <= row_radius).astype(jnp.float32)
    for q in range(8):
        re = jnp.concatenate([win_ref[o, 0, q], win_ref[o, 0, q + 1]], axis=1)
        im = jnp.concatenate([win_ref[o, 1, q], win_ref[o, 1, q + 1]], axis=1)
        mask = (jnp.abs(lane // 16 - 8) <= col_radius(q)).astype(jnp.float32)
        mask = (mask * row_mask).astype(jnp.bfloat16)
        left = jnp.concatenate([re * mask, im * mask], axis=1)
        real = lax.dot_general(left, jnp.concatenate([re, im], axis=1), dims, preferred_element_type=jnp.float32)
        imag = lax.dot_general(left, jnp.concatenate([-im, re], axis=1), dims, preferred_element_type=jnp.float32)
        only = jnp.where(diagonal, real, 0.0)
        power_n = jnp.sum(only, axis=0, keepdims=True)
        power_m = jnp.sum(only, axis=1, keepdims=True)
        scale_n = jnp.where(power_n > 0, lax.rsqrt(power_n), 0.0) * CODE
        scale_m = jnp.where(power_m > 0, lax.rsqrt(power_m), 0.0)
        high = power_n.astype(jnp.bfloat16).astype(jnp.float32)
        code_real = jnp.where(spare, high, jnp.exp2(real * scale_m * scale_n))
        code_imag = jnp.where(spare, power_n - high, jnp.exp2(imag * scale_m * scale_n))
        store(q, code_real.astype(jnp.bfloat16).reshape(8, 16, 128), code_imag.astype(jnp.bfloat16).reshape(8, 16, 128))


def stack_kernel(
    raw_hbm, line_ref, offset_ref, slope_ref, row_radius_ref, col_radius_ref, out_ref,
    raw_ref, packed_ref, slots_ref, edges_ref, before_ref, after_ref, lines_ref, win_ref, code_ref,
    group_sem, raw_sem, send_sem, recv_sem, own_sem, edge_send, edge_recv, code_send, code_recv, code_own,
):
    acq, strip = lax.axis_index("acq"), lax.axis_index("strip")
    place = (acq, strip)
    mesh_id = pl.DeviceIdType.MESH

    def device(to):
        return {"acq": to[0], "strip": to[1]}

    barrier = pltpu.get_barrier_semaphore()

    def greet(semaphore, to):
        pl.semaphore_signal(semaphore, inc=1, device_id=device(to), device_id_type=mesh_id)

    for i in range(1, N_STRIP):
        greet(barrier, shift(place, i, 0))
    for n in range(1, N_GROUP):
        greet(barrier, shift(place, 0, n))

    def fetch(s):
        return pltpu.make_async_copy(raw_hbm.at[s], raw_ref.at[s], raw_sem.at[s])

    def fetch_start(i, carry):
        fetch(shift(place, strip_step(i), 0)[1]).start()
        return carry

    lax.fori_loop(0, N_STRIP, fetch_start, 0)
    squared = offset_ref[...].astype(jnp.float32) ** 2
    lines = line_ref[...].astype(jnp.float32)
    reader_lane = lax.broadcasted_iota(jnp.int32, (CAP, N_STRIP), 1)

    def pack(i, carry):
        s = shift(place, strip_step(i), 0)[1]
        fetch(s).wait()
        mine = reader_lane == s
        column = jnp.sum(jnp.where(mine, squared, 0.0), axis=1, keepdims=True)
        line = jnp.sum(jnp.where(mine, lines, 0.0), axis=1, keepdims=True)
        pack_strip(raw_ref, packed_ref, s, line, column * slope_ref[...])
        return carry

    lax.fori_loop(0, 2, pack, 0)
    pl.semaphore_wait(barrier, N_STRIP + N_GROUP - 2)
    for n in range(1, N_GROUP):
        greet(group_sem, shift(place, 0, n))
    lax.fori_loop(2, EARLY, pack, 0)
    pl.semaphore_wait(group_sem, N_GROUP - 1)

    own = pltpu.make_async_copy(packed_ref.at[acq, strip], slots_ref.at[acq, strip], own_sem)

    def slot_copy(n, i):
        to = shift(place, strip_step(i), acq_step(n))
        return pltpu.make_async_remote_copy(
            src_ref=packed_ref.at[to[0], to[1]],
            dst_ref=slots_ref.at[acq, strip],
            send_sem=send_sem.at[n * N_STRIP + i],
            recv_sem=recv_sem.at[n],
            device_id=device(to),
            device_id_type=mesh_id,
        )

    def send(n, i):
        @pl.when(n * N_STRIP + i > 0)
        def _():
            slot_copy(n, i).start()

    def send_pair(first):
        def body(i, carry):
            send(first, i)
            send(first + 1, i)
            return carry

        return body

    def pack_and_send(i, carry):
        pack(i, carry)
        return send_pair(0)(i, carry)

    lax.fori_loop(0, EARLY, send_pair(0), 0)
    lax.fori_loop(EARLY, N_STRIP, pack_and_send, 0)
    own.start()
    for first in (2, 4, 6):
        lax.fori_loop(0, N_STRIP, send_pair(first), 0)

    def source(n):
        return shift(place, 0, acq_back(acq_step(n)))[0]

    def edge_copy(up):
        to = (strip + (1 if up else N_STRIP - 1)) % N_STRIP
        return pltpu.make_async_remote_copy(
            src_ref=edges_ref,
            dst_ref=before_ref if up else after_ref,
            send_sem=edge_send.at[1 if up else 0],
            recv_sem=edge_recv.at[1 if up else 0],
            device_id=device((acq, to)),
            device_id_type=mesh_id,
        )

    def rows_of(a):
        return pl.ds(pl.multiple_of(a * 16, 16), 16)

    def arrival(n, a, count):
        return pltpu.make_async_remote_copy(
            src_ref=packed_ref.at[a, pl.ds(0, count)],
            dst_ref=slots_ref.at[a, pl.ds(0, count)],
            send_sem=send_sem.at[n],
            recv_sem=recv_sem.at[n],
            device_id=device((acq, (strip + 1) % N_STRIP)),
            device_id_type=mesh_id,
        )

    def slots_of(a):
        return slots_ref[a].astype(jnp.float32).reshape(N_STRIP * CAP, PIECE).astype(jnp.bfloat16)

    def block(n, carry):
        a = source(n)

        @pl.when(n == 0)
        def _():
            own.wait()
            arrival(n, a, N_STRIP - 1).wait_recv()

        @pl.when(n > 0)
        def _():
            arrival(n, a, N_STRIP).wait_recv()

        slots = slots_of(a)

        def store(part, cols, value):
            for o in range(8):
                win_ref[o, part, cols, rows_of(a), :] = turned(value[o], o)

        regroup(slots, window_picks(slots), lines_ref, store)
        return carry

    lax.fori_loop(0, N_GROUP, block, 0)

    def code_copy(n, o):
        to = shift(place, 0, acq_step(n))
        return pltpu.make_async_remote_copy(
            src_ref=code_ref.at[o, to[0]],
            dst_ref=out_ref.at[acq, o],
            send_sem=code_send.at[n, o],
            recv_sem=code_recv.at[n, o],
            device_id=device(to),
            device_id_type=mesh_id,
        )

    def code_keep(o):
        return pltpu.make_async_copy(code_ref.at[o, acq], out_ref.at[acq, o], code_own.at[o])

    def line(o, carry):
        def store(q, code_real, code_imag):
            code_ref[o, :, q, :, 0:128] = code_real
            code_ref[o, :, q, :, 128:256] = code_imag

        gram(win_ref, row_radius_ref[o], lambda q: col_radius_ref[acq * 8 + q], o, store)
        for n in (6, 1, 7, 2, 5, 3, 4):
            code_copy(n, o).start()
        code_keep(o).start()
        return carry

    line(1, 0)

    def edge(a, carry):
        edges_ref[a] = edge_rows(slots_of(a))
        return carry

    lax.fori_loop(0, N_GROUP, edge, 0)
    edge_copy(True).start()
    edge_copy(False).start()
    lax.fori_loop(2, 7, line, 0)

    edge_copy(True).wait_recv()
    edge_copy(False).wait_recv()
    picks = border_picks(jnp.where(strip > 0, 1.0, 0.0), jnp.where(strip < N_STRIP - 1, 1.0, 0.0))

    def border(a, carry):
        def store(part, cols, value):
            for o in (0, 7):
                win_ref[o, part, cols, rows_of(a), :] += turned(value[o], o)

        regroup(jnp.concatenate([before_ref[a], after_ref[a]], axis=0), picks, lines_ref, store)
        return carry

    lax.fori_loop(0, N_GROUP, border, 0)
    line(0, 0)
    line(7, 0)

    def sent(j, carry):
        slot_copy(j // N_STRIP, j % N_STRIP).wait_send()
        return carry

    lax.fori_loop(1, N_GROUP * N_STRIP, sent, 0)
    edge_copy(True).wait_send()
    edge_copy(False).wait_send()

    def finish(j, carry):
        o = (j + 1) % 7 + 6 * (j // 7)
        code_keep(o).wait()
        for n in range(1, N_GROUP):
            code_copy(n, o).wait()
        return carry

    lax.fori_loop(0, 8, finish, 0)


def place_kernel(code_hbm, out_ref, flat_ref, power_ref, code_ref, code_sem):
    step = pl.program_id(0)

    @pl.when(step == 0)
    def _():
        def fetch(o):
            rows = pl.ds(o * 8, 8)
            return pltpu.make_async_copy(code_hbm.at[:, rows], code_ref.at[:, rows], code_sem.at[o])

        for o in range(8):
            fetch(o).start()
        for o in range(8):
            fetch(o).wait()
            for g in range(8):
                at = (o * 64 + g * 8) * 16
                block = code_ref[g, o * 8 : o * 8 + 8].astype(jnp.float32)
                block = block.reshape(128, 256)
                flat_ref[0, at : at + 128, :] = block[:, :128]
                flat_ref[1, at : at + 128, :] = block[:, 128:]
        high = flat_ref[0, pl.ds(15, 512, stride=16), :]
        rest = flat_ref[1, pl.ds(15, 512, stride=16), :]
        power_ref[...] = (high + rest).T

    power_n = power_ref[...]
    root_n = jnp.sqrt(power_n)
    for j in range(PLACE):
        m = step * PLACE + j
        me = lax.axis_index("acq") * 16 + m
        power_m = power_ref[pl.ds(me, 1), :]
        scale = root_n * jnp.sqrt(power_m) * lax.rsqrt(power_n * power_m + epsilon) * (1.0 / CODE)
        for part in range(2):
            codes = flat_ref[part, pl.ds(m, 512, stride=16), :].T
            scaled = jnp.log2(codes) * scale
            for block in range(8):
                for t in range(4):
                    piece = scaled[block * 16 : block * 16 + ACQ_LOC, t * 128 : t * 128 + 128]
                    out_ref[j, pl.ds(block * ACQ_LOC * 8 + t * 2 + part, ACQ_LOC, stride=8), :] = piece


def per_device(
    raw_echo_values,
    cell_target_line,
    cell_track_displacement,
    along_track_chirp_slope,
    along_track_look_radius,
    range_look_radius,
):
    f32, bf16 = jnp.float32, jnp.bfloat16
    raw = raw_echo_values.reshape(N_STRIP, CAP, ACQ_LOC, 2, 4, 128)
    raw = raw.transpose(0, 1, 2, 4, 3, 5).reshape(N_STRIP, CAP * ACQ_LOC * 8, 128)
    dma = pltpu.SemaphoreType.DMA
    received = pl.pallas_call(
        stack_kernel,
        out_shape=jax.ShapeDtypeStruct((N_GROUP, 8, 8, 16, 256), bf16),
        in_specs=[
            pl.BlockSpec(memory_space=pl.ANY),
            pl.BlockSpec(memory_space=pltpu.VMEM),
            pl.BlockSpec(memory_space=pltpu.VMEM),
            pl.BlockSpec(memory_space=pltpu.VMEM),
            pl.BlockSpec(memory_space=pltpu.SMEM),
            pl.BlockSpec(memory_space=pltpu.SMEM),
        ],
        out_specs=pl.BlockSpec(memory_space=pl.ANY),
        scratch_shapes=[
            pltpu.VMEM((N_STRIP, CAP * ACQ_LOC * 8, 128), f32),
            pltpu.VMEM((N_GROUP, N_STRIP, CAP, PIECE), bf16),
            pltpu.VMEM((N_GROUP, N_STRIP, CAP, PIECE), bf16),
            pltpu.VMEM((N_GROUP, 16, PIECE), bf16),
            pltpu.VMEM((N_GROUP, 16, PIECE), bf16),
            pltpu.VMEM((N_GROUP, 16, PIECE), bf16),
            pltpu.VMEM((PIECE, 128), f32),
            pltpu.VMEM((8, 2, 9, 128, 128), bf16),
            pltpu.VMEM((8, N_GROUP, 8, 16, 256), bf16),
            pltpu.SemaphoreType.REGULAR,
            dma((N_STRIP,)),
            dma((N_GROUP * N_STRIP,)),
            dma((N_GROUP,)),
            dma,
            dma((2,)),
            dma((2,)),
            dma((N_GROUP, 8)),
            dma((N_GROUP, 8)),
            dma((8,)),
        ],
        compiler_params=pltpu.CompilerParams(vmem_limit_bytes=VMEM, collective_id=0, has_side_effects=True),
        name="stack",
    )(
        raw,
        cell_target_line[0].T,
        cell_track_displacement[0].T,
        along_track_chirp_slope[None],
        along_track_look_radius,
        range_look_radius,
    )
    received = received.reshape(N_GROUP, 64, 16, 256)
    placed = pl.pallas_call(
        place_kernel,
        grid=(ACQ_LOC // PLACE,),
        out_shape=jax.ShapeDtypeStruct((ACQ_LOC, 960, 128), f32),
        in_specs=[pl.BlockSpec(memory_space=pl.ANY)],
        out_specs=pl.BlockSpec((PLACE, 960, 128), lambda m: (m, 0, 0)),
        scratch_shapes=[
            pltpu.VMEM((2, 512 * 16, 128), f32),
            pltpu.VMEM((128, 512), f32),
            pltpu.VMEM((8, 64, 16, 256), bf16),
            dma((8,)),
        ],
        compiler_params=params(),
        name="place",
    )(received)
    placed = placed.reshape(ACQ_LOC, 120, 4, 2, 128).transpose(0, 1, 3, 2, 4)
    return placed.reshape(ACQ_LOC, 120, 2, 512)


def solution(mesh):
    placed = (
        P("strip", None, None, "acq", None, None),
        P("strip", None, None),
        P("strip", None, None),
        P("acq"),
        P("strip"),
        P(),
    )
    return jax.shard_map(
        per_device,
        mesh=mesh,
        in_specs=placed,
        out_specs=P("acq", None, None, "strip"),
        check_vma=False,
    )
```
